128 devices in a mesh: lon: 16 (over z_lo, x, core), lat: 8 (over z_hi, y).
Axes of the slice: x: 4, y: 4, z: 4 (z_hi: 2, z_lo: 2; z = z_hi * 2 + z_lo), core: 2. Of those that a mesh axis runs over, the one named last changes fastest.
Arguments:
- tracers: float32 [8, 1440, 72, 128], P('lat', 'lon'), may hold values from -6 to 6
- offsets: int32 [8], P('lat'), may hold values from -180 to 180, as said below
- fraction: float32 [8], P('lat'), may hold values from 0 to 1
- cutoffs: int32 [8], P('lat'), may hold values from 1 to 48, as said below
- keep_high: float32 [8], P('lat'), may hold values from 0.1 to 0.5
- mixing: float32 [8], P('lat'), may hold values from 0.05 to 0.24
- kz: float32 [8, 1440, 72], P('lat', 'lon'), may hold values from 0.05 to 20
- light: float32 [8, 1440], P('lat', 'lon'), may hold values from 0.2 to 1.5
- loss_rate: float32 [72, 128], replicated, may hold values from 0.02 to 4
- source: float32 [72, 128], replicated, may hold values from -3 to 3
Outputs:
- updated: float32 [8, 1440, 72, 128], P('lat', 'lon')
The draws below stay inside these ranges and needn't reach their ends.
Inputs may be any that keep to these rules, and one draw needn't show every extreme that they name: `offsets`: row r's offset has magnitude at most 180 * min(r + 2, 8) // 8; row 7 has offset 180 and row 6 has offset -180. `cutoffs`: row 0 keeps 48 wavenumbers and row 7 keeps 1.
All inputs are finite; a program needn't handle non-finite values.
Results may differ from the reference program's by a relative error of at most 0.0003.
Values sent between devices are 32-bit elements; how exact they have to be, the bound alone decides.
A program may use at most 64 MiB of HBM per device.

```python
import math
import jax
import jax.numpy as jnp
from jax import lax

NLON = 1440
LEV = 72
NTR = 128
KMAX = 48
NLAT = 8
SMAX = 180


def draw_offsets(key, part):
    row_index = lax.iota(jnp.int32, NLAT)
    row_bound = SMAX * jnp.minimum(row_index + 2, NLAT) // NLAT
    size_key, sign_key = jax.random.split(key)
    magnitude = jax.random.randint(size_key, (NLAT,), 0, row_bound + 1)
    sign_factor = 2 * jax.random.randint(sign_key, (NLAT,), 0, 2) - 1
    values = magnitude * sign_factor
    values = values.at[NLAT - 1].set(SMAX)
    values = values.at[NLAT - 2].set(-SMAX)
    return values.astype(jnp.int32)


def draw_cutoffs(key, part):
    values = jax.random.randint(key, (NLAT,), 1, KMAX + 1)
    values = values.at[0].set(KMAX)
    values = values.at[NLAT - 1].set(1)
    return values.astype(jnp.int32)


def block_levels(rng, shape, cuts, smallest, high):
    def one(axis_at, parts):
        draws = jax.random.uniform(jax.random.fold_in(jax.random.fold_in(rng, 6), axis_at), (parts,), jnp.float32, smallest / len(cuts), high / len(cuts))
        return jnp.repeat(jnp.exp(draws), shape[axis_at] // parts).reshape((-1,) + (1,) * (len(shape) - axis_at - 1))

    level = one(*cuts[0])
    for cut in cuts[1:]:
        level = level * one(*cut)
    return level


def bell_draw(rng, shape, deviation, limit, shards=(), held_as=jnp.bfloat16):
    entries = jax.random.normal(rng, shape, jnp.float32) * deviation
    if len(shards) > 0:
        entries = block_levels(rng, shape, shards, -0.22, 0.18) * entries
    return jnp.clip(entries, min=-limit, max=limit).astype(held_as)


def setup_inputs(seed: int = 0) -> dict:
    key_list = jax.random.split(jax.random.key(seed), 11)
    tracers = bell_draw(key_list[0], (NLAT, NLON, LEV, NTR), 1.0, 6.0, ((0, 8), (1, 16)), jnp.float32)
    offsets = draw_offsets(jax.random.fold_in(key_list[10], 71), 0)
    fraction = jnp.clip(1.0 * jax.random.uniform(key_list[2], (NLAT,), jnp.float32) ** block_levels(key_list[2], (NLAT,), ((0, 8),), -0.2, 0.2), 0.0, 1.0)
    cutoffs = draw_cutoffs(jax.random.fold_in(key_list[10], 71), 0)
    keep_high = jnp.clip(0.1 + 0.4 * jax.random.uniform(key_list[4], (NLAT,), jnp.float32) ** block_levels(key_list[4], (NLAT,), ((0, 8),), -0.2, 0.2), 0.1, 0.5)
    mixing = jnp.clip(0.05 + 0.19 * jax.random.uniform(key_list[5], (NLAT,), jnp.float32) ** block_levels(key_list[5], (NLAT,), ((0, 8),), -0.2, 0.2), 0.05, 0.24)
    kz = jnp.clip(jnp.exp(math.log(20.0) - 5.9914645 * jax.random.uniform(key_list[6], (NLAT, NLON, LEV), jnp.float32) ** block_levels(key_list[6], (NLAT, NLON, LEV), ((0, 8), (1, 16)), -0.2, 0.2)), 0.05, 20.0)
    light = jnp.clip(0.2 + 1.3 * jax.random.uniform(key_list[7], (NLAT, NLON), jnp.float32) ** block_levels(key_list[7], (NLAT, NLON), ((0, 8), (1, 16)), -0.2, 0.2), 0.2, 1.5)
    loss_rate = jnp.clip(jnp.exp(jax.random.uniform(key_list[8], (LEV, NTR), jnp.float32, math.log(0.02), math.log(4.0))), 0.02, 4.0)
    source = bell_draw(key_list[9], (LEV, NTR), 0.5, 3.0, (), jnp.float32)
    return {"tracers": tracers, "offsets": offsets, "fraction": fraction, "cutoffs": cutoffs, "keep_high": keep_high, "mixing": mixing, "kz": kz, "light": light, "loss_rate": loss_rate, "source": source}


def column_solve(field, coupling):
    nothing = jnp.zeros_like(coupling[..., :1])
    above = jnp.concatenate([coupling[..., 1:], nothing], axis=-1)
    below = jnp.concatenate([nothing, -coupling[..., 1:]], axis=-1)
    return lax.linalg.tridiagonal_solve(below, 1.0 + coupling + above, -above, field)

def reference(tracers, offsets, fraction, cutoffs, keep_high, mixing, kz, light, loss_rate, source):
    settled = column_solve(tracers, kz).reshape(NLAT, NLON, LEV * NTR)

    def one_latitude(packed):
        circle, amount, weight, highest, keep_factor = packed
        moved = (1.0 - weight) * jnp.roll(circle, amount, axis=0) + weight * jnp.roll(circle, amount + 1, axis=0)
        spectrum = jnp.fft.rfft(moved, axis=0)
        waves = jnp.arange(NLON // 2 + 1)
        spectrum = jnp.where((waves <= highest)[:, None], spectrum, 0)
        lowpass = jnp.fft.irfft(spectrum, n=NLON, axis=0)
        return keep_factor * moved + (1.0 - keep_factor) * lowpass
    filtered = lax.map(one_latitude, (settled, offsets, fraction, cutoffs, keep_high))
    extended = jnp.pad(filtered, ((1, 1), (0, 0), (0, 0)), mode='edge')
    spread = filtered + mixing[:, None, None] * (extended[:-2] + extended[2:] - 2.0 * filtered)
    spread = spread.reshape(NLAT, NLON, LEV, NTR)
    glow = light[:, :, None, None]
    return (spread + source * glow) / (1.0 + loss_rate * glow)
```

```python
import functools
import math

import jax
import jax.numpy as jnp
import numpy as np
from jax import lax
from jax.experimental import pallas as pl
from jax.experimental.pallas import tpu as pltpu
from jax.sharding import PartitionSpec as P

NLON = 1440
KMAX = 48
MESH = pl.DeviceIdType.MESH
CELLS = 90
PEERS = 8
HALF = CELLS * PEERS
TILES = 9
EDGE = 184
KPAD = 56
LEFT = EDGE
RIGHT = EDGE + HALF


def split_bf16(table):
    import ml_dtypes

    high = table.astype(ml_dtypes.bfloat16)
    low = (table - high.astype(np.float64)).astype(ml_dtypes.bfloat16)
    return high, low


def wave_tables():
    places = np.arange(HALF)
    waves = np.arange(KMAX + 1)
    phase = (places[:, None] * waves[None, :] % NLON) * (2.0 * math.pi / NLON)
    table = np.zeros((HALF, 2 * KPAD))
    table[:, : KMAX + 1] = np.cos(phase)
    table[:, KPAD : KPAD + KMAX + 1] = np.sin(phase)
    high, low = split_bf16(table)
    rebuild = np.concatenate([high, low], axis=1)
    project = np.ascontiguousarray(rebuild.T)
    shifts = np.arange(-EDGE, EDGE)
    phase = (shifts[:, None] * waves[None, :] % NLON) * (2.0 * math.pi / NLON)
    turn = np.zeros((2 * EDGE, 128), np.float32)
    turn[:, : KMAX + 1] = np.cos(phase)
    turn[:, KPAD : KPAD + KMAX + 1] = np.sin(phase)
    return project, rebuild, turn


def kernel(
    off_ref,
    frac_ref,
    cut_ref,
    keep_ref,
    mix_ref,
    light_ref,
    tracers_ref,
    kz_ref,
    loss_ref,
    source_ref,
    project_ref,
    rebuild_ref,
    turn_ref,
    out_ref,
    inp,
    kbuf,
    glow,
    rot,
    dp,
    cp,
    got,
    circ,
    edge,
    edge_in,
    spec,
    spec_in,
    rows,
    back,
    outb,
    in_sem,
    fs,
    fr,
    es,
    er,
    ss,
    sr,
    ls,
    lr,
    bs,
    br,
    out_sem,
):
    lon = lax.axis_index("lon")
    lat = lax.axis_index("lat")
    me = lon % PEERS
    base = lon - me
    other = {"lon": (lon + PEERS) % (2 * PEERS), "lat": lat}
    has_south = lat > 0
    has_north = lat < 7

    def peer(p):
        return {"lon": base + p, "lat": lat}

    def tile_in(j):
        return pltpu.make_async_copy(
            tracers_ref.at[:, pl.ds(pl.multiple_of(j * 8, 8), 8), :], inp.at[j], in_sem.at[j]
        )

    def tile_out(j):
        return pltpu.make_async_copy(
            outb.at[j], out_ref.at[:, pl.ds(pl.multiple_of(j * 8, 8), 8), :], out_sem.at[j]
        )

    def forth(j, src, dst, to):
        return pltpu.make_async_remote_copy(
            dp.at[j, src], got.at[j, dst], fs.at[j, src], fr.at[j, dst],
            device_id=peer(to), device_id_type=MESH,
        )

    def home(j, src, dst, to):
        return pltpu.make_async_remote_copy(
            got.at[j, src], back.at[j, dst], bs.at[j, src], br.at[j, dst],
            device_id=peer(to), device_id_type=MESH,
        )

    def edge_copy(j):
        return pltpu.make_async_remote_copy(
            edge.at[j], edge_in.at[j], es.at[j], er.at[j],
            device_id=other, device_id_type=MESH,
        )

    def spec_copy(j):
        return pltpu.make_async_remote_copy(
            spec.at[j], spec_in.at[j], ss.at[j], sr.at[j],
            device_id=other, device_id_type=MESH,
        )

    def row_copy(j, slot, to):
        return pltpu.make_async_remote_copy(
            rows.at[2, j], rows.at[slot, j], ls.at[slot, j], lr.at[slot, j],
            device_id={"lon": lon, "lat": to}, device_id_type=MESH,
        )

    def start_in(j, carry):
        tile_in(j).start()
        return carry

    lax.fori_loop(0, TILES, start_in, 0)

    barrier = pltpu.get_barrier_semaphore()
    for d in range(1, PEERS):
        pl.semaphore_signal(barrier, inc=1, device_id=peer((me + d) % PEERS), device_id_type=MESH)
    pl.semaphore_signal(barrier, inc=1, device_id=other, device_id_type=MESH)

    @pl.when(has_south)
    def _():
        pl.semaphore_signal(
            barrier, inc=1, device_id={"lon": lon, "lat": lat - 1}, device_id_type=MESH
        )

    @pl.when(has_north)
    def _():
        pl.semaphore_signal(
            barrier, inc=1, device_id={"lon": lon, "lat": lat + 1}, device_id_type=MESH
        )

    off = off_ref[0]
    frac = frac_ref[0]
    keep = keep_ref[0]
    mix = mix_ref[0]
    kbuf[...] = jnp.zeros_like(kbuf)
    kbuf[:, 0:72] = kz_ref[...]

    def light_row(c, carry):
        glow[pl.ds(c, 1), :] = jnp.full((1, 128), light_ref[0, c], jnp.float32)
        return carry

    lax.fori_loop(0, CELLS, light_row, 0)

    lane = lax.broadcasted_iota(jnp.int32, (1, 128), 1)
    wave = lane % KPAD
    share = jnp.where(wave <= cut_ref[0], jnp.where(wave == 0, 1.0, 2.0) / NLON, 0.0) * (1.0 - keep)
    turn = (1.0 - frac) * turn_ref[pl.ds(EDGE + off, 1), :] + frac * turn_ref[pl.ds(EDGE + 1 + off, 1), :]
    rot[...] = jnp.broadcast_to(turn * share, (128, 128)).T

    def down(j, carry):
        last, e, kc = carry
        tile_in(j).wait()
        flat = inp.at[j].reshape(CELLS * 8, 128)
        kr = pltpu.roll(kbuf[...], lax.rem(128 - 8 * j, 128), 1)
        for p in range(8):
            kn = jnp.broadcast_to(kr[:, p + 1 : p + 2], (CELLS, 128))
            g = 1.0 + kc * e
            inv = 1.0 / (g + kn)
            last = (flat[pl.ds(p, CELLS, stride=8), :] + kc * last) * inv
            e = g * inv
            dp[j, p] = last
            cp[j, p] = kn * inv
            kc = kn
        return last, e, kc

    zero = jnp.zeros((CELLS, 128), jnp.float32)
    lax.fori_loop(
        0, TILES, down, (zero, zero + 1.0, jnp.broadcast_to(kbuf[:, 0:1], (CELLS, 128)))
    )

    @pl.when(has_south & has_north)
    def _():
        pl.semaphore_wait(barrier, PEERS + 2)

    @pl.when(jnp.logical_not(has_south & has_north))
    def _():
        pl.semaphore_wait(barrier, PEERS + 1)

    def up(c, x):
        j = TILES - 1 - c
        for p in reversed(range(8)):
            x = dp[j, p] + cp[j, p] * x
            dp[j, p] = x
        for d in range(1, PEERS):
            to = (me + d) % PEERS
            forth(j, to, me, to).start()
        pltpu.make_async_copy(dp.at[j, me], got.at[j, me], fr.at[j, me]).start()
        return x

    lax.fori_loop(0, TILES, up, zero)

    def gather(j):
        for d in range(1, PEERS):
            s = (me + d) % PEERS
            forth(j, s, s, s).wait_recv()
        pltpu.make_async_copy(dp.at[j, me], got.at[j, me], fr.at[j, me]).wait()
        for s in range(PEERS):
            circ[j, LEFT + CELLS * s : LEFT + CELLS * (s + 1), :] = got[j, s]
        begin = jnp.clip(LEFT + (off + 1) * (HALF - EDGE), LEFT, RIGHT - EDGE)
        edge[j] = circ[j, pl.ds(begin, EDGE), :]
        edge_copy(j).start()
        field = circ[j, LEFT:RIGHT, :]
        high = field.astype(jnp.bfloat16)
        low = (field - high.astype(jnp.float32)).astype(jnp.bfloat16)
        part = jnp.dot(
            project_ref[...], jnp.concatenate([high, low], axis=1), preferred_element_type=jnp.float32
        )
        n = 2 * KPAD
        spec[j] = part[:n, :128] + part[n:, :128] + part[:n, 128:]
        spec_copy(j).start()

    def filt(j):
        edge_copy(j).wait_recv()
        taken = edge_in[j]
        circ[j, 0:EDGE, :] = taken
        circ[j, RIGHT : RIGHT + EDGE, :] = taken
        spec_copy(j).wait_recv()
        level = lax.broadcasted_iota(jnp.int32, (KPAD, 128), 0)
        sign = jnp.where(level % 2 == 0, 1.0, -1.0)
        a = spec[j, 0:KPAD, :] + sign * spec_in[j, 0:KPAD, :]
        b = spec[j, KPAD : 2 * KPAD, :] + sign * spec_in[j, KPAD : 2 * KPAD, :]
        c = rot[0:KPAD, :]
        d = rot[KPAD : 2 * KPAD, :]
        turned = jnp.concatenate([c * a - d * b, d * a + c * b], axis=0)
        high = turned.astype(jnp.bfloat16)
        low = (turned - high.astype(jnp.float32)).astype(jnp.bfloat16)
        weight = jnp.concatenate(
            [
                jnp.concatenate([high, low], axis=1),
                jnp.concatenate([high, jnp.zeros_like(low)], axis=1),
            ],
            axis=0,
        )
        block = HALF // 3
        for s in range(3):
            lowpass = jnp.dot(
                rebuild_ref[s * block : (s + 1) * block, :], weight, preferred_element_type=jnp.float32
            )
            near = circ[j, pl.ds(LEFT + s * block - off, block), :]
            far = circ[j, pl.ds(LEFT + s * block - 1 - off, block), :]
            moved = (1.0 - frac) * near + frac * far
            rows[2, j, s * block : (s + 1) * block, :] = (
                keep * moved + lowpass[:, :128] + lowpass[:, 128:]
            )

        @pl.when(has_north)
        def _():
            row_copy(j, 0, lat + 1).start()

        @pl.when(has_south)
        def _():
            row_copy(j, 1, lat - 1).start()

    south_slot = jnp.where(has_south, 0, 2)
    north_slot = jnp.where(has_north, 1, 2)

    def spread(j):
        @pl.when(has_south)
        def _():
            row_copy(j, 0, lat - 1).wait_recv()

        @pl.when(has_north)
        def _():
            row_copy(j, 1, lat + 1).wait_recv()

        for s in range(PEERS):
            part = pl.ds(CELLS * s, CELLS)
            got[j, s] = (1.0 - 2.0 * mix) * rows[2, j, part, :] + mix * (
                rows[south_slot, j, part, :] + rows[north_slot, j, part, :]
            )
        for d in range(1, PEERS):
            to = (me + d) % PEERS
            home(j, to, me, to).start()
        pltpu.make_async_copy(got.at[j, me], back.at[j, me], br.at[j, me]).start()

    def finish(j):
        for d in range(1, PEERS):
            s = (me + d) % PEERS
            home(j, s, s, s).wait_recv()
        pltpu.make_async_copy(got.at[j, me], back.at[j, me], br.at[j, me]).wait()
        flat = outb.at[j].reshape(CELLS * 8, 128)
        light = glow[...]
        for p in range(PEERS):
            level = j * 8 + p
            top = back[j, p] + source_ref[pl.ds(level, 1), :] * light
            flat[pl.ds(p, CELLS, stride=8), :] = top / (1.0 + loss_ref[pl.ds(level, 1), :] * light)
        tile_out(j).start()

    stages = ((gather, 0), (filt, 1), (spread, 3), (finish, 4))

    def step(t, carry):
        for stage, lag in stages:

            @pl.when((t >= lag) & (t < lag + TILES))
            def _():
                stage(TILES - 1 - (t - lag))

        return carry

    lax.fori_loop(0, TILES + stages[-1][1], step, 0)

    def drain(j, carry):
        for d in range(1, PEERS):
            to = (me + d) % PEERS
            forth(j, to, me, to).wait_send()
            home(j, to, me, to).wait_send()
        edge_copy(j).wait_send()
        spec_copy(j).wait_send()

        @pl.when(has_north)
        def _():
            row_copy(j, 0, lat + 1).wait_send()

        @pl.when(has_south)
        def _():
            row_copy(j, 1, lat - 1).wait_send()

        tile_out(j).wait()
        return carry

    lax.fori_loop(0, TILES, drain, 0)


def body(tracers, offsets, fraction, cutoffs, keep_high, mixing, kz, light, loss_rate, source):
    project, rebuild, turn = wave_tables()
    levels, species = tracers.shape[2:]
    smem = pl.BlockSpec(memory_space=pltpu.SMEM)
    vmem = pl.BlockSpec(memory_space=pltpu.VMEM)
    hbm = pl.BlockSpec(memory_space=pl.ANY)
    f32 = jnp.float32
    dma = pltpu.SemaphoreType.DMA
    out = pl.pallas_call(
        kernel,
        out_shape=jax.ShapeDtypeStruct((CELLS, levels, species), f32),
        in_specs=[smem] * 6 + [hbm] + [vmem] * 6,
        out_specs=hbm,
        scratch_shapes=[
            pltpu.VMEM((TILES, CELLS, 8, 128), f32),
            pltpu.VMEM((CELLS, 128), f32),
            pltpu.VMEM((CELLS, 128), f32),
            pltpu.VMEM((128, 128), f32),
            pltpu.VMEM((TILES, PEERS, CELLS, 128), f32),
            pltpu.VMEM((TILES, PEERS, CELLS, 128), f32),
            pltpu.VMEM((TILES, PEERS, CELLS, 128), f32),
            pltpu.VMEM((TILES, HALF + 2 * EDGE, 128), f32),
            pltpu.VMEM((TILES, EDGE, 128), f32),
            pltpu.VMEM((TILES, EDGE, 128), f32),
            pltpu.VMEM((TILES, 2 * KPAD, 128), f32),
            pltpu.VMEM((TILES, 2 * KPAD, 128), f32),
            pltpu.VMEM((3, TILES, HALF, 128), f32),
            pltpu.VMEM((TILES, PEERS, CELLS, 128), f32),
            pltpu.VMEM((TILES, CELLS, 8, 128), f32),
            dma((TILES,)),
            dma((TILES, PEERS)),
            dma((TILES, PEERS)),
            dma((TILES,)),
            dma((TILES,)),
            dma((TILES,)),
            dma((TILES,)),
            dma((2, TILES)),
            dma((2, TILES)),
            dma((TILES, PEERS)),
            dma((TILES, PEERS)),
            dma((TILES,)),
        ],
        compiler_params=pltpu.CompilerParams(
            collective_id=0, has_side_effects=True, vmem_limit_bytes=58 << 20
        ),
        name="transport",
    )(
        offsets,
        fraction,
        cutoffs,
        keep_high,
        mixing,
        light,
        tracers.reshape(CELLS, levels, species),
        kz.reshape(CELLS, levels),
        loss_rate,
        source,
        jnp.asarray(project),
        jnp.asarray(rebuild),
        jnp.asarray(turn),
    )
    return out.reshape(tracers.shape)


def solution(mesh):
    return jax.shard_map(
        body,
        mesh=mesh,
        in_specs=(
            P("lat", "lon", None, None),
            P("lat"),
            P("lat"),
            P("lat"),
            P("lat"),
            P("lat"),
            P("lat", "lon", None),
            P("lat", "lon"),
            P(),
            P(),
        ),
        out_specs=P("lat", "lon", None, None),
        check_vma=False,
    )
```

```python
import functools
import math

import jax
import jax.numpy as jnp
import numpy as np
from jax import lax
from jax.experimental import pallas as pl
from jax.experimental.pallas import tpu as pltpu
from jax.sharding import PartitionSpec as P

NLON = 1440
KMAX = 48
MESH = pl.DeviceIdType.MESH
CELLS = 90
PEERS = 8
HALF = CELLS * PEERS
TILES = 9
EDGE = 184
KPAD = 56
DIRECT = 360
RELAYED = ((3, 7), (7, 3), (7, 4), (4, 7), (4, 0), (0, 4), (0, 3), (3, 0))
LEFT = EDGE
RIGHT = EDGE + HALF


def split_bf16(table):
    import ml_dtypes

    high = table.astype(ml_dtypes.bfloat16)
    low = (table - high.astype(np.float64)).astype(ml_dtypes.bfloat16)
    return high, low


def wave_tables():
    places = np.arange(HALF)
    waves = np.arange(KMAX + 1)
    phase = (places[:, None] * waves[None, :] % NLON) * (2.0 * math.pi / NLON)
    table = np.zeros((HALF, 2 * KPAD))
    table[:, : KMAX + 1] = np.cos(phase)
    table[:, KPAD : KPAD + KMAX + 1] = np.sin(phase)
    high, low = split_bf16(table)
    rebuild = np.concatenate([high, low], axis=1)
    project = np.ascontiguousarray(rebuild.T)
    shifts = np.arange(-EDGE, EDGE)
    phase = (shifts[:, None] * waves[None, :] % NLON) * (2.0 * math.pi / NLON)
    turn = np.zeros((2 * EDGE, 128), np.float32)
    turn[:, : KMAX + 1] = np.cos(phase)
    turn[:, KPAD : KPAD + KMAX + 1] = np.sin(phase)
    return project, rebuild, turn


def kernel(
    off_ref,
    frac_ref,
    cut_ref,
    keep_ref,
    mix_ref,
    light_ref,
    tracers_ref,
    kz_ref,
    loss_ref,
    source_ref,
    project_ref,
    rebuild_ref,
    turn_ref,
    out_ref,
    inp,
    kbuf,
    glow,
    rot,
    dp,
    cp,
    got,
    circ,
    edge,
    edge_in,
    spec,
    spec_in,
    rows,
    relay,
    back,
    outb,
    in_sem,
    fs,
    fr,
    es,
    er,
    ss,
    sr,
    ls,
    lr,
    rs,
    rr,
    os,
    orr,
    bs,
    br,
    out_sem,
):
    lon = lax.axis_index("lon")
    lat = lax.axis_index("lat")
    me = lon % PEERS
    base = lon - me
    other = {"lon": (lon + PEERS) % (2 * PEERS), "lat": lat}
    has_south = lat > 0
    has_north = lat < 7
    plain_south = has_south & (lat != 4)
    plain_north = has_north & (lat != 3)

    def peer(p):
        return {"lon": base + p, "lat": lat}

    def tile_in(j):
        return pltpu.make_async_copy(
            tracers_ref.at[:, pl.ds(pl.multiple_of(j * 8, 8), 8), :], inp.at[j], in_sem.at[j]
        )

    def tile_out(j):
        return pltpu.make_async_copy(
            outb.at[j], out_ref.at[:, pl.ds(pl.multiple_of(j * 8, 8), 8), :], out_sem.at[j]
        )

    def forth(j, src, dst, to):
        return pltpu.make_async_remote_copy(
            dp.at[j, src], got.at[j, dst], fs.at[j, src], fr.at[j, dst],
            device_id=peer(to), device_id_type=MESH,
        )

    def home(j, src, dst, to):
        return pltpu.make_async_remote_copy(
            got.at[j, src], back.at[j, dst], bs.at[j, src], br.at[j, dst],
            device_id=peer(to), device_id_type=MESH,
        )

    def edge_copy(j):
        return pltpu.make_async_remote_copy(
            edge.at[j], edge_in.at[j], es.at[j], er.at[j],
            device_id=other, device_id_type=MESH,
        )

    def spec_copy(j):
        return pltpu.make_async_remote_copy(
            spec.at[j], spec_in.at[j], ss.at[j], sr.at[j],
            device_id=other, device_id_type=MESH,
        )

    def row_copy(j, slot, to):
        return pltpu.make_async_remote_copy(
            rows.at[2, j], rows.at[slot, j], ls.at[slot, j], lr.at[slot, j],
            device_id={"lon": lon, "lat": to}, device_id_type=MESH,
        )

    def half_copy(j, slot, to):
        return pltpu.make_async_remote_copy(
            rows.at[2, j, pl.ds(0, DIRECT)], rows.at[slot, j, pl.ds(0, DIRECT)],
            ls.at[slot, j], lr.at[slot, j],
            device_id={"lon": lon, "lat": to}, device_id_type=MESH,
        )

    def relay_copy(j, to):
        return pltpu.make_async_remote_copy(
            rows.at[2, j, pl.ds(DIRECT, HALF - DIRECT)], relay.at[j], rs.at[j], rr.at[j],
            device_id={"lon": lon, "lat": to}, device_id_type=MESH,
        )

    def onward_copy(j, slot, to):
        return pltpu.make_async_remote_copy(
            relay.at[j], rows.at[slot, j, pl.ds(DIRECT, HALF - DIRECT)], os.at[j], orr.at[j],
            device_id={"lon": lon, "lat": to}, device_id_type=MESH,
        )

    def start_in(j, carry):
        tile_in(j).start()
        return carry

    lax.fori_loop(0, TILES, start_in, 0)

    barrier = pltpu.get_barrier_semaphore()
    for d in range(1, PEERS):
        pl.semaphore_signal(barrier, inc=1, device_id=peer((me + d) % PEERS), device_id_type=MESH)
    pl.semaphore_signal(barrier, inc=1, device_id=other, device_id_type=MESH)

    @pl.when(has_south)
    def _():
        pl.semaphore_signal(
            barrier, inc=1, device_id={"lon": lon, "lat": lat - 1}, device_id_type=MESH
        )

    @pl.when(has_north)
    def _():
        pl.semaphore_signal(
            barrier, inc=1, device_id={"lon": lon, "lat": lat + 1}, device_id_type=MESH
        )

    for here, there in RELAYED:

        @pl.when(lat == here)
        def _():
            pl.semaphore_signal(
                barrier, inc=1, device_id={"lon": lon, "lat": there}, device_id_type=MESH
            )

    off = off_ref[0]
    frac = frac_ref[0]
    keep = keep_ref[0]
    mix = mix_ref[0]
    rot[...] = jnp.zeros_like(rot)
    rot[0:72, 0:CELLS] = kz_ref[...]
    kbuf[...] = rot[...].T[0:CELLS, :]

    def light_row(c, carry):
        glow[pl.ds(c, 1), :] = jnp.full((1, 128), light_ref[0, c], jnp.float32)
        return carry

    lax.fori_loop(0, CELLS, light_row, 0)

    lane = lax.broadcasted_iota(jnp.int32, (1, 128), 1)
    wave = lane % KPAD
    share = jnp.where(wave <= cut_ref[0], jnp.where(wave == 0, 1.0, 2.0) / NLON, 0.0) * (1.0 - keep)
    turn = (1.0 - frac) * turn_ref[pl.ds(EDGE + off, 1), :] + frac * turn_ref[pl.ds(EDGE + 1 + off, 1), :]
    rot[...] = jnp.broadcast_to(turn * share, (128, 128)).T

    def down(j, carry):
        last, e, kc = carry
        tile_in(j).wait()
        flat = inp.at[j].reshape(CELLS * 8, 128)
        kr = pltpu.roll(kbuf[...], lax.rem(128 - 8 * j, 128), 1)
        for p in range(8):
            kn = jnp.broadcast_to(kr[:, p + 1 : p + 2], (CELLS, 128))
            g = 1.0 + kc * e
            inv = 1.0 / (g + kn)
            last = (flat[pl.ds(p, CELLS, stride=8), :] + kc * last) * inv
            e = g * inv
            dp[j, p] = last
            cp[j, p] = kn * inv
            kc = kn
        return last, e, kc

    zero = jnp.zeros((CELLS, 128), jnp.float32)
    lax.fori_loop(
        0, TILES, down, (zero, zero + 1.0, jnp.broadcast_to(kbuf[:, 0:1], (CELLS, 128)))
    )

    edge_row = (lat == 0) | (lat == 7)
    cross_row = (lat == 3) | (lat == 4)

    @pl.when(edge_row)
    def _():
        pl.semaphore_wait(barrier, PEERS + 3)

    @pl.when(cross_row)
    def _():
        pl.semaphore_wait(barrier, PEERS + 4)

    @pl.when(jnp.logical_not(edge_row | cross_row))
    def _():
        pl.semaphore_wait(barrier, PEERS + 2)

    def up(c, x):
        j = TILES - 1 - c
        for p in reversed(range(8)):
            x = dp[j, p] + cp[j, p] * x
            dp[j, p] = x

        @pl.when(c == 0)
        def _():
            send(j)

        return x

    def send(j):
        for d in range(1, PEERS):
            to = (me + d) % PEERS
            forth(j, to, me, to).start()
        pltpu.make_async_copy(dp.at[j, me], got.at[j, me], fr.at[j, me]).start()

    lax.fori_loop(0, TILES, up, zero)

    def gather(j):
        for d in range(1, PEERS):
            s = (me + d) % PEERS
            forth(j, s, s, s).wait_recv()
        pltpu.make_async_copy(dp.at[j, me], got.at[j, me], fr.at[j, me]).wait()

        @pl.when(j == TILES - 1)
        def _():
            send(j - 1)

        @pl.when(j >= 2)
        def _():
            send(j - 2)

        for s in range(PEERS):
            circ[j, LEFT + CELLS * s : LEFT + CELLS * (s + 1), :] = got[j, s]
        begin = jnp.clip(LEFT + (off + 1) * (HALF - EDGE), LEFT, RIGHT - EDGE)
        edge[j] = circ[j, pl.ds(begin, EDGE), :]
        edge_copy(j).start()
        field = circ[j, LEFT:RIGHT, :]
        high = field.astype(jnp.bfloat16)
        low = (field - high.astype(jnp.float32)).astype(jnp.bfloat16)
        part = jnp.dot(
            project_ref[...], jnp.concatenate([high, low], axis=1), preferred_element_type=jnp.float32
        )
        n = 2 * KPAD
        spec[j] = part[:n, :128] + part[n:, :128] + part[:n, 128:]
        spec_copy(j).start()

    def filt(j):
        edge_copy(j).wait_recv()
        taken = edge_in[j]
        circ[j, 0:EDGE, :] = taken
        circ[j, RIGHT : RIGHT + EDGE, :] = taken
        spec_copy(j).wait_recv()
        level = lax.broadcasted_iota(jnp.int32, (KPAD, 128), 0)
        sign = jnp.where(level % 2 == 0, 1.0, -1.0)
        a = spec[j, 0:KPAD, :] + sign * spec_in[j, 0:KPAD, :]
        b = spec[j, KPAD : 2 * KPAD, :] + sign * spec_in[j, KPAD : 2 * KPAD, :]
        c = rot[0:KPAD, :]
        d = rot[KPAD : 2 * KPAD, :]
        turned = jnp.concatenate([c * a - d * b, d * a + c * b], axis=0)
        high = turned.astype(jnp.bfloat16)
        low = (turned - high.astype(jnp.float32)).astype(jnp.bfloat16)
        weight = jnp.concatenate(
            [
                jnp.concatenate([high, low], axis=1),
                jnp.concatenate([high, jnp.zeros_like(low)], axis=1),
            ],
            axis=0,
        )
        block = HALF // 3
        for s in range(3):
            lowpass = jnp.dot(
                rebuild_ref[s * block : (s + 1) * block, :], weight, preferred_element_type=jnp.float32
            )
            near = circ[j, pl.ds(LEFT + s * block - off, block), :]
            far = circ[j, pl.ds(LEFT + s * block - 1 - off, block), :]
            moved = (1.0 - frac) * near + frac * far
            rows[2, j, s * block : (s + 1) * block, :] = (
                keep * moved + lowpass[:, :128] + lowpass[:, 128:]
            )

        @pl.when(lat == 3)
        def _():
            half_copy(j, 0, 4).start()
            relay_copy(j, 7).start()

        @pl.when(lat == 4)
        def _():
            half_copy(j, 1, 3).start()
            relay_copy(j, 0).start()

        @pl.when(plain_north)
        def _():
            row_copy(j, 0, lat + 1).start()

        @pl.when(plain_south)
        def _():
            row_copy(j, 1, lat - 1).start()

    def onward(j):
        @pl.when(lat == 7)
        def _():
            relay_copy(j, 7).wait_recv()
            onward_copy(j, 0, 4).start()

        @pl.when(lat == 0)
        def _():
            relay_copy(j, 0).wait_recv()
            onward_copy(j, 1, 3).start()

    south_slot = jnp.where(has_south, 0, 2)
    north_slot = jnp.where(has_north, 1, 2)

    def spread(j):
        @pl.when(plain_south)
        def _():
            row_copy(j, 0, lat - 1).wait_recv()

        @pl.when(plain_north)
        def _():
            row_copy(j, 1, lat + 1).wait_recv()

        @pl.when(lat == 4)
        def _():
            half_copy(j, 0, 3).wait_recv()
            onward_copy(j, 0, 7).wait_recv()

        @pl.when(lat == 3)
        def _():
            half_copy(j, 1, 4).wait_recv()
            onward_copy(j, 1, 0).wait_recv()

        for s in range(PEERS):
            part = pl.ds(CELLS * s, CELLS)
            got[j, s] = (1.0 - 2.0 * mix) * rows[2, j, part, :] + mix * (
                rows[south_slot, j, part, :] + rows[north_slot, j, part, :]
            )
        for d in range(1, PEERS):
            to = (me + d) % PEERS
            home(j, to, me, to).start()
        pltpu.make_async_copy(got.at[j, me], back.at[j, me], br.at[j, me]).start()

    def finish(j):
        for d in range(1, PEERS):
            s = (me + d) % PEERS
            home(j, s, s, s).wait_recv()
        pltpu.make_async_copy(got.at[j, me], back.at[j, me], br.at[j, me]).wait()
        flat = outb.at[j].reshape(CELLS * 8, 128)
        light = glow[...]
        for p in range(PEERS):
            level = j * 8 + p
            top = back[j, p] + source_ref[pl.ds(level, 1), :] * light
            flat[pl.ds(p, CELLS, stride=8), :] = top / (1.0 + loss_ref[pl.ds(level, 1), :] * light)
        tile_out(j).start()

    stages = ((filt, 2), (onward, 3), (gather, 0), (finish, 4), (spread, 3))

    def step(t, carry):
        for stage, lag in stages:

            @pl.when((t >= lag) & (t < lag + TILES))
            def _():
                stage(TILES - 1 - (t - lag))

        return carry

    lax.fori_loop(0, TILES + 4, step, 0)

    def drain(j, carry):
        for d in range(1, PEERS):
            to = (me + d) % PEERS
            forth(j, to, me, to).wait_send()
            home(j, to, me, to).wait_send()
        edge_copy(j).wait_send()
        spec_copy(j).wait_send()

        @pl.when(plain_north)
        def _():
            row_copy(j, 0, lat + 1).wait_send()

        @pl.when(plain_south)
        def _():
            row_copy(j, 1, lat - 1).wait_send()

        @pl.when(lat == 3)
        def _():
            half_copy(j, 0, 4).wait_send()
            relay_copy(j, 7).wait_send()

        @pl.when(lat == 4)
        def _():
            half_copy(j, 1, 3).wait_send()
            relay_copy(j, 0).wait_send()

        @pl.when(lat == 7)
        def _():
            onward_copy(j, 0, 4).wait_send()

        @pl.when(lat == 0)
        def _():
            onward_copy(j, 1, 3).wait_send()

        tile_out(j).wait()
        return carry

    lax.fori_loop(0, TILES, drain, 0)


def body(tracers, offsets, fraction, cutoffs, keep_high, mixing, kz, light, loss_rate, source):
    project, rebuild, turn = wave_tables()
    levels, species = tracers.shape[2:]
    smem = pl.BlockSpec(memory_space=pltpu.SMEM)
    vmem = pl.BlockSpec(memory_space=pltpu.VMEM)
    hbm = pl.BlockSpec(memory_space=pl.ANY)
    f32 = jnp.float32
    dma = pltpu.SemaphoreType.DMA
    out = pl.pallas_call(
        kernel,
        out_shape=jax.ShapeDtypeStruct((CELLS, levels, species), f32),
        in_specs=[smem] * 6 + [hbm] + [vmem] * 6,
        out_specs=hbm,
        scratch_shapes=[
            pltpu.VMEM((TILES, CELLS, 8, 128), f32),
            pltpu.VMEM((CELLS, 128), f32),
            pltpu.VMEM((CELLS, 128), f32),
            pltpu.VMEM((128, 128), f32),
            pltpu.VMEM((TILES, PEERS, CELLS, 128), f32),
            pltpu.VMEM((TILES, PEERS, CELLS, 128), f32),
            pltpu.VMEM((TILES, PEERS, CELLS, 128), f32),
            pltpu.VMEM((TILES, HALF + 2 * EDGE, 128), f32),
            pltpu.VMEM((TILES, EDGE, 128), f32),
            pltpu.VMEM((TILES, EDGE, 128), f32),
            pltpu.VMEM((TILES, 2 * KPAD, 128), f32),
            pltpu.VMEM((TILES, 2 * KPAD, 128), f32),
            pltpu.VMEM((3, TILES, HALF, 128), f32),
            pltpu.VMEM((TILES, HALF - DIRECT, 128), f32),
            pltpu.VMEM((TILES, PEERS, CELLS, 128), f32),
            pltpu.VMEM((TILES, CELLS, 8, 128), f32),
            dma((TILES,)),
            dma((TILES, PEERS)),
            dma((TILES, PEERS)),
            dma((TILES,)),
            dma((TILES,)),
            dma((TILES,)),
            dma((TILES,)),
            dma((2, TILES)),
            dma((2, TILES)),
            dma((TILES,)),
            dma((TILES,)),
            dma((TILES,)),
            dma((TILES,)),
            dma((TILES, PEERS)),
            dma((TILES, PEERS)),
            dma((TILES,)),
        ],
        compiler_params=pltpu.CompilerParams(
            collective_id=0, has_side_effects=True, vmem_limit_bytes=58 << 20
        ),
        name="transport",
    )(
        offsets,
        fraction,
        cutoffs,
        keep_high,
        mixing,
        light,
        tracers.reshape(CELLS, levels, species),
        kz.reshape(CELLS, levels).T,
        loss_rate,
        source,
        jnp.asarray(project),
        jnp.asarray(rebuild),
        jnp.asarray(turn),
    )
    return out.reshape(tracers.shape)


def solution(mesh):
    return jax.shard_map(
        body,
        mesh=mesh,
        in_specs=(
            P("lat", "lon", None, None),
            P("lat"),
            P("lat"),
            P("lat"),
            P("lat"),
            P("lat"),
            P("lat", "lon", None),
            P("lat", "lon"),
            P(),
            P(),
        ),
        out_specs=P("lat", "lon", None, None),
        check_vma=False,
    )
```

```python
import functools
import math

import jax
import jax.numpy as jnp
import numpy as np
from jax import lax
from jax.experimental import pallas as pl
from jax.experimental.pallas import tpu as pltpu
from jax.sharding import PartitionSpec as P

NLON = 1440
KMAX = 48
MESH = pl.DeviceIdType.MESH
CELLS = 90
PEERS = 8
HALF = CELLS * PEERS
LEVELS = 72
TILES = 9
EDGE = 184
KPAD = 56
DIRECT = HALF // 2
GROUP = PEERS // 2
RELAYED = ((3, 7), (7, 3), (7, 4), (4, 7), (4, 0), (0, 4), (0, 3), (3, 0))
LEFT = EDGE
RIGHT = EDGE + HALF


def split_bf16(table):
    import ml_dtypes

    high = table.astype(ml_dtypes.bfloat16)
    low = (table - high.astype(np.float64)).astype(ml_dtypes.bfloat16)
    return high, low


def wave_tables():
    places = np.arange(HALF)
    waves = np.arange(KMAX + 1)
    phase = (places[:, None] * waves[None, :] % NLON) * (2.0 * math.pi / NLON)
    table = np.zeros((HALF, 2 * KPAD))
    table[:, : KMAX + 1] = np.cos(phase)
    table[:, KPAD : KPAD + KMAX + 1] = np.sin(phase)
    high, low = split_bf16(table)
    rebuild = np.concatenate([high, low], axis=1)
    project = np.ascontiguousarray(rebuild.T)
    shifts = np.arange(-EDGE, EDGE)
    phase = (shifts[:, None] * waves[None, :] % NLON) * (2.0 * math.pi / NLON)
    turn = np.zeros((2 * EDGE, 128), np.float32)
    turn[:, : KMAX + 1] = np.cos(phase)
    turn[:, KPAD : KPAD + KMAX + 1] = np.sin(phase)
    return project, rebuild, turn


def kernel(
    off_hbm,
    frac_hbm,
    cut_hbm,
    keep_hbm,
    mix_hbm,
    light_hbm,
    tracers_ref,
    kz_hbm,
    turn_hbm,
    project_hbm,
    rebuild_hbm,
    loss_hbm,
    source_hbm,
    out_ref,
    off_ref,
    frac_ref,
    cut_ref,
    keep_ref,
    mix_ref,
    light_ref,
    kz_ref,
    turn_ref,
    project_ref,
    rebuild_ref,
    loss_ref,
    source_ref,
    inp,
    kbuf,
    glow,
    rot,
    dp,
    cp,
    got,
    circ,
    given,
    taken,
    rows,
    relay,
    back,
    in_sem,
    fs,
    fr,
    es,
    ss,
    er,
    ls,
    lr,
    rs,
    rr,
    os,
    bs,
    br,
    arg_sem,
):
    lon = lax.axis_index("lon")
    lat = lax.axis_index("lat")
    me = lon % PEERS
    base = lon - me
    other = {"lon": (lon + PEERS) % (2 * PEERS), "lat": lat}
    has_south = lat > 0
    has_north = lat < 7
    plain_south = has_south & (lat != 4)
    plain_north = has_north & (lat != 3)

    def peer(p):
        return {"lon": base + p, "lat": lat}

    def tile_in(j):
        return pltpu.make_async_copy(
            tracers_ref.at[:, pl.ds(pl.multiple_of(j * 8, 8), 8), :], inp.at[j], in_sem.at[j]
        )

    def forth(j, src, dst, to):
        return pltpu.make_async_remote_copy(
            dp.at[j, src], got.at[j, dst], fs, fr.at[j], device_id=peer(to), device_id_type=MESH
        )

    def home(j, src, dst, to):
        return pltpu.make_async_remote_copy(
            got.at[j, src], back.at[j, dst], bs, br.at[j], device_id=peer(to), device_id_type=MESH
        )

    def edge_copy(j):
        return pltpu.make_async_remote_copy(
            given.at[j, pl.ds(0, EDGE)], taken.at[j, pl.ds(0, EDGE)], es, er.at[j],
            device_id=other, device_id_type=MESH,
        )

    def spec_copy(j):
        return pltpu.make_async_remote_copy(
            given.at[j, pl.ds(EDGE, 2 * KPAD)], taken.at[j, pl.ds(EDGE, 2 * KPAD)], ss, er.at[j],
            device_id=other, device_id_type=MESH,
        )

    def half(h):
        return pl.ds(h * DIRECT, DIRECT)

    def row_copy(j, h, slot, to):
        return pltpu.make_async_remote_copy(
            rows.at[2, j, half(h)], rows.at[slot, j, half(h)], ls.at[slot], lr.at[slot, h, j],
            device_id={"lon": lon, "lat": to}, device_id_type=MESH,
        )

    def relay_copy(j, to):
        return pltpu.make_async_remote_copy(
            rows.at[2, j, half(1)], relay.at[j], rs, rr.at[j],
            device_id={"lon": lon, "lat": to}, device_id_type=MESH,
        )

    def onward_copy(j, slot, to):
        return pltpu.make_async_remote_copy(
            relay.at[j], rows.at[slot, j, half(1)], os, lr.at[slot, 1, j],
            device_id={"lon": lon, "lat": to}, device_id_type=MESH,
        )

    def start_in(j, carry):
        tile_in(j).start()
        return carry

    pairs = (
        (kz_hbm, kz_ref),
        (off_hbm, off_ref),
        (frac_hbm, frac_ref),
        (cut_hbm, cut_ref),
        (keep_hbm, keep_ref),
        (mix_hbm, mix_ref),
        (light_hbm, light_ref),
        (turn_hbm, turn_ref),
        (project_hbm, project_ref),
        (rebuild_hbm, rebuild_ref),
        (loss_hbm, loss_ref),
        (source_hbm, source_ref),
    )
    arrivals = [
        pltpu.make_async_copy(src, dst, arg_sem.at[n]) for n, (src, dst) in enumerate(pairs)
    ]
    arrivals[0].start()
    lax.fori_loop(0, TILES, start_in, 0)
    for copy in arrivals[1:]:
        copy.start()

    barrier = pltpu.get_barrier_semaphore()
    for d in range(1, PEERS):
        pl.semaphore_signal(barrier, inc=1, device_id=peer((me + d) % PEERS), device_id_type=MESH)
    pl.semaphore_signal(barrier, inc=1, device_id=other, device_id_type=MESH)

    @pl.when(has_south)
    def _():
        pl.semaphore_signal(
            barrier, inc=1, device_id={"lon": lon, "lat": lat - 1}, device_id_type=MESH
        )

    @pl.when(has_north)
    def _():
        pl.semaphore_signal(
            barrier, inc=1, device_id={"lon": lon, "lat": lat + 1}, device_id_type=MESH
        )

    for here, there in RELAYED:

        @pl.when(lat == here)
        def _():
            pl.semaphore_signal(
                barrier, inc=1, device_id={"lon": lon, "lat": there}, device_id_type=MESH
            )

    arrivals[0].wait()
    rot[...] = jnp.zeros_like(rot)
    rot[0:72, 0:CELLS] = kz_ref[...]
    kbuf[...] = rot[...].T[0:CELLS, :]

    def down(j, carry):
        last, e, kc = carry
        tile_in(j).wait()
        flat = inp.at[j].reshape(CELLS * 8, 128)
        kr = pltpu.roll(kbuf[...], lax.rem(128 - 8 * j, 128), 1)
        for p in range(8):
            kn = jnp.broadcast_to(kr[:, p + 1 : p + 2], (CELLS, 128))
            g = 1.0 + kc * e
            inv = 1.0 / (g + kn)
            last = (flat[pl.ds(p, CELLS, stride=8), :] + kc * last) * inv
            e = g * inv
            dp[j, p] = last
            cp[j, p] = kn * inv
            kc = kn
        return last, e, kc

    zero = jnp.zeros((CELLS, 128), jnp.float32)
    lax.fori_loop(
        0, TILES, down, (zero, zero + 1.0, jnp.broadcast_to(kbuf[:, 0:1], (CELLS, 128)))
    )

    edge_row = (lat == 0) | (lat == 7)
    cross_row = (lat == 3) | (lat == 4)

    @pl.when(edge_row)
    def _():
        pl.semaphore_wait(barrier, PEERS + 3)

    @pl.when(cross_row)
    def _():
        pl.semaphore_wait(barrier, PEERS + 4)

    @pl.when(jnp.logical_not(edge_row | cross_row))
    def _():
        pl.semaphore_wait(barrier, PEERS + 2)

    def up(c, x):
        j = TILES - 1 - c
        for p in reversed(range(8)):
            x = dp[j, p] + cp[j, p] * x
            dp[j, p] = x

        @pl.when(c == 0)
        def _():
            send(j)

        return x

    def send(j):
        for d in range(1, PEERS):
            to = (me + d) % PEERS
            forth(j, to, me, to).start()
        pltpu.make_async_copy(dp.at[j, me], got.at[j, me], fr.at[j]).start()

    lax.fori_loop(0, TILES, up, zero)

    for copy in arrivals[1:]:
        copy.wait()
    off = off_ref[0]
    frac = frac_ref[0]
    keep = keep_ref[0]
    mix = mix_ref[0]

    def light_row(c, carry):
        glow[pl.ds(c, 1), :] = jnp.full((1, 128), light_ref[0, c], jnp.float32)
        return carry

    lax.fori_loop(0, CELLS, light_row, 0)

    lane = lax.broadcasted_iota(jnp.int32, (1, 128), 1)
    wave = lane % KPAD
    share = jnp.where(wave <= cut_ref[0], jnp.where(wave == 0, 1.0, 2.0) / NLON, 0.0) * (1.0 - keep)
    turn = (1.0 - frac) * turn_ref[pl.ds(EDGE + off, 1), :] + frac * turn_ref[pl.ds(EDGE + 1 + off, 1), :]
    rot[...] = jnp.broadcast_to(turn * share, (128, 128)).T

    def gather(j):
        pltpu.make_async_copy(dp.at[j], got.at[j], fr.at[j]).wait()

        @pl.when(j == TILES - 1)
        def _():
            send(j - 1)

        @pl.when(j >= 2)
        def _():
            send(j - 2)

        for s in range(PEERS):
            circ[j, LEFT + CELLS * s : LEFT + CELLS * (s + 1), :] = got[j, s]
        begin = jnp.clip(LEFT + (off + 1) * (HALF - EDGE), LEFT, RIGHT - EDGE)
        given[j, 0:EDGE, :] = circ[j, pl.ds(begin, EDGE), :]
        edge_copy(j).start()
        field = circ[j, LEFT:RIGHT, :]
        high = field.astype(jnp.bfloat16)
        low = (field - high.astype(jnp.float32)).astype(jnp.bfloat16)
        part = jnp.dot(
            project_ref[...], jnp.concatenate([high, low], axis=1), preferred_element_type=jnp.float32
        )
        n = 2 * KPAD
        given[j, EDGE : EDGE + n, :] = part[:n, :128] + part[n:, :128] + part[:n, 128:]
        spec_copy(j).start()

    def filt(j):
        pltpu.make_async_copy(given.at[j], taken.at[j], er.at[j]).wait()
        fresh = taken[j, 0:EDGE, :]
        circ[j, 0:EDGE, :] = fresh
        circ[j, RIGHT : RIGHT + EDGE, :] = fresh
        level = lax.broadcasted_iota(jnp.int32, (KPAD, 128), 0)
        sign = jnp.where(level % 2 == 0, 1.0, -1.0)
        cosine, sine = slice(EDGE, EDGE + KPAD), slice(EDGE + KPAD, EDGE + 2 * KPAD)
        a = given[j, cosine, :] + sign * taken[j, cosine, :]
        b = given[j, sine, :] + sign * taken[j, sine, :]
        c = rot[0:KPAD, :]
        d = rot[KPAD : 2 * KPAD, :]
        turned = jnp.concatenate([c * a - d * b, d * a + c * b], axis=0)
        high = turned.astype(jnp.bfloat16)
        low = (turned - high.astype(jnp.float32)).astype(jnp.bfloat16)
        weight = jnp.concatenate(
            [
                jnp.concatenate([high, low], axis=1),
                jnp.concatenate([high, jnp.zeros_like(low)], axis=1),
            ],
            axis=0,
        )
        for h in range(2):
            first = h * DIRECT
            lowpass = jnp.dot(
                rebuild_ref[first : first + DIRECT, :], weight, preferred_element_type=jnp.float32
            )
            near = circ[j, pl.ds(LEFT + first - off, DIRECT), :]
            far = circ[j, pl.ds(LEFT + first - 1 - off, DIRECT), :]
            moved = (1.0 - frac) * near + frac * far
            rows[2, j, first : first + DIRECT, :] = keep * moved + lowpass[:, :128] + lowpass[:, 128:]

            @pl.when(plain_north)
            def _():
                row_copy(j, h, 0, lat + 1).start()

            @pl.when(plain_south)
            def _():
                row_copy(j, h, 1, lat - 1).start()

            @pl.when(lat == 3)
            def _():
                (relay_copy(j, 7) if h else row_copy(j, 0, 0, 4)).start()

            @pl.when(lat == 4)
            def _():
                (relay_copy(j, 0) if h else row_copy(j, 0, 1, 3)).start()

    def onward(j):
        @pl.when(lat == 7)
        def _():
            relay_copy(j, 7).wait_recv()
            onward_copy(j, 0, 4).start()

        @pl.when(lat == 0)
        def _():
            relay_copy(j, 0).wait_recv()
            onward_copy(j, 1, 3).start()

    south_slot = jnp.where(has_south, 0, 2)
    north_slot = jnp.where(has_north, 1, 2)

    def spread(j):
        for h in range(2):

            @pl.when(has_south)
            def _():
                row_copy(j, h, 0, lat - 1).wait_recv()

            @pl.when(has_north)
            def _():
                row_copy(j, h, 1, lat + 1).wait_recv()

            for s in range(h * GROUP, (h + 1) * GROUP):
                part = pl.ds(CELLS * s, CELLS)
                got[j, s] = (1.0 - 2.0 * mix) * rows[2, j, part, :] + mix * (
                    rows[south_slot, j, part, :] + rows[north_slot, j, part, :]
                )
            for d in range(1, GROUP):
                to = h * GROUP + (me + d) % GROUP
                home(j, to, me, to).start()

            @pl.when(me // GROUP == h)
            def _():
                pltpu.make_async_copy(got.at[j, me], back.at[j, me], br.at[j]).start()

            @pl.when(me // GROUP != h)
            def _():
                to = h * GROUP + me % GROUP
                home(j, to, me, to).start()

    def finish(j):
        pltpu.make_async_copy(got.at[j], back.at[j], br.at[j]).wait()
        flat = out_ref.reshape(CELLS * LEVELS, 128)
        light = glow[...]
        for p in range(PEERS):
            level = j * 8 + p
            top = back[j, p] + source_ref[pl.ds(level, 1), :] * light
            flat[pl.ds(level, CELLS, stride=LEVELS), :] = top / (
                1.0 + loss_ref[pl.ds(level, 1), :] * light
            )

    stages = ((filt, 2), (gather, 0), (onward, 2), (finish, 4), (spread, 3))

    def step(t, carry):
        for stage, lag in stages:

            @pl.when((t >= lag) & (t < lag + TILES))
            def _():
                stage(TILES - 1 - (t - lag))

        return carry

    lax.fori_loop(0, TILES + 4, step, 0)

    sent = pl.ds(0, PEERS - 1)
    pltpu.make_async_copy(dp.at[:, sent], dp.at[:, sent], fs).wait()
    pltpu.make_async_copy(got.at[:, sent], got.at[:, sent], bs).wait()
    edges, spectra = pl.ds(0, EDGE), pl.ds(EDGE, 2 * KPAD)
    pltpu.make_async_copy(given.at[:, edges], given.at[:, edges], es).wait()
    pltpu.make_async_copy(given.at[:, spectra], given.at[:, spectra], ss).wait()
    whole, part = rows.at[2], rows.at[2, :, half(0)]

    @pl.when(plain_north)
    def _():
        pltpu.make_async_copy(whole, whole, ls.at[0]).wait()

    @pl.when(plain_south)
    def _():
        pltpu.make_async_copy(whole, whole, ls.at[1]).wait()

    @pl.when(lat == 3)
    def _():
        pltpu.make_async_copy(part, part, ls.at[0]).wait()

    @pl.when(lat == 4)
    def _():
        pltpu.make_async_copy(part, part, ls.at[1]).wait()

    @pl.when(cross_row)
    def _():
        pltpu.make_async_copy(relay, relay, rs).wait()

    @pl.when(edge_row)
    def _():
        pltpu.make_async_copy(relay, relay, os).wait()


def body(tracers, offsets, fraction, cutoffs, keep_high, mixing, kz, light, loss_rate, source):
    project, rebuild, turn = wave_tables()
    levels, species = tracers.shape[2:]
    hbm = pl.BlockSpec(memory_space=pltpu.HBM)
    f32 = jnp.float32
    dma = pltpu.SemaphoreType.DMA
    operands = (
        offsets,
        fraction,
        cutoffs,
        keep_high,
        mixing,
        light,
        tracers.reshape(CELLS, levels, species),
        kz.reshape(CELLS, levels).T,
        jnp.asarray(turn),
        jnp.asarray(project),
        jnp.asarray(rebuild),
        loss_rate,
        source,
    )
    out = pl.pallas_call(
        kernel,
        out_shape=pltpu.VMEM((CELLS, levels, species), f32),
        in_specs=[hbm] * 13,
        out_specs=pl.BlockSpec(memory_space=pltpu.VMEM),
        scratch_shapes=[
            pltpu.SMEM((1,), jnp.int32),
            pltpu.SMEM((1,), f32),
            pltpu.SMEM((1,), jnp.int32),
            pltpu.SMEM((1,), f32),
            pltpu.SMEM((1,), f32),
            pltpu.SMEM((1, CELLS), f32),
            pltpu.VMEM((levels, CELLS), f32),
            pltpu.VMEM(turn.shape, f32),
            pltpu.VMEM(project.shape, jnp.bfloat16),
            pltpu.VMEM(rebuild.shape, jnp.bfloat16),
            pltpu.VMEM((levels, species), f32),
            pltpu.VMEM((levels, species), f32),
            pltpu.VMEM((TILES, CELLS, 8, 128), f32),
            pltpu.VMEM((CELLS, 128), f32),
            pltpu.VMEM((CELLS, 128), f32),
            pltpu.VMEM((128, 128), f32),
            pltpu.VMEM((TILES, PEERS, CELLS, 128), f32),
            pltpu.VMEM((TILES, PEERS, CELLS, 128), f32),
            pltpu.VMEM((TILES, PEERS, CELLS, 128), f32),
            pltpu.VMEM((TILES, HALF + 2 * EDGE, 128), f32),
            pltpu.VMEM((TILES, EDGE + 2 * KPAD, 128), f32),
            pltpu.VMEM((TILES, EDGE + 2 * KPAD, 128), f32),
            pltpu.VMEM((3, TILES, HALF, 128), f32),
            pltpu.VMEM((TILES, DIRECT, 128), f32),
            pltpu.VMEM((TILES, PEERS, CELLS, 128), f32),
            dma((TILES,)),
            dma,
            dma((TILES,)),
            dma,
            dma,
            dma((TILES,)),
            dma((2,)),
            dma((2, 2, TILES)),
            dma,
            dma((TILES,)),
            dma,
            dma,
            dma((TILES,)),
            dma((12,)),
        ],
        compiler_params=pltpu.CompilerParams(
            collective_id=0, has_side_effects=True, vmem_limit_bytes=46 << 20
        ),
        name="transport",
    )(*[pltpu.with_memory_space_constraint(x, pltpu.HBM) if x.size > 1 else x for x in operands])
    return out.reshape(tracers.shape)


def solution(mesh):
    return jax.shard_map(
        body,
        mesh=mesh,
        in_specs=(
            P("lat", "lon", None, None),
            P("lat"),
            P("lat"),
            P("lat"),
            P("lat"),
            P("lat"),
            P("lat", "lon", None),
            P("lat", "lon"),
            P(),
            P(),
        ),
        out_specs=P("lat", "lon", None, None),
        check_vma=False,
    )
```

```python
import functools
import math

import jax
import jax.numpy as jnp
import numpy as np
from jax import lax
from jax.experimental import pallas as pl
from jax.experimental.pallas import tpu as pltpu
from jax.sharding import PartitionSpec as P

NLON = 1440
KMAX = 48
MESH = pl.DeviceIdType.MESH
CELLS = 90
PEERS = 8
HALF = CELLS * PEERS
LEVELS = 72
TILES = 9
EDGE = 184
KPAD = 56
DIRECT = HALF // 2
GROUP = PEERS // 2
RELAYED = ((3, 7), (7, 3), (7, 4), (4, 7), (4, 0), (0, 4), (0, 3), (3, 0))
LOW = 8
FULL = ((0, 2 * KPAD),)
CLASSES = (
    (0, 0, 48, FULL),
    (1, 2, 96, FULL),
    (3, 4, 136, FULL),
    (5, 6, EDGE, FULL),
    (7, 7, EDGE, ((0, LOW), (KPAD, LOW))),
)
LEFT = EDGE
RIGHT = EDGE + HALF


def split_bf16(table):
    import ml_dtypes

    high = table.astype(ml_dtypes.bfloat16)
    low = (table - high.astype(np.float64)).astype(ml_dtypes.bfloat16)
    return high, low


def wave_tables():
    places = np.arange(HALF)
    waves = np.arange(KMAX + 1)
    phase = (places[:, None] * waves[None, :] % NLON) * (2.0 * math.pi / NLON)
    table = np.zeros((HALF, 2 * KPAD))
    table[:, : KMAX + 1] = np.cos(phase)
    table[:, KPAD : KPAD + KMAX + 1] = np.sin(phase)
    high, low = split_bf16(table)
    rebuild = np.concatenate([high, low], axis=1)
    project = np.ascontiguousarray(rebuild.T)
    shifts = np.arange(-EDGE, EDGE)
    phase = (shifts[:, None] * waves[None, :] % NLON) * (2.0 * math.pi / NLON)
    turn = np.zeros((2 * EDGE, 128), np.float32)
    turn[:, : KMAX + 1] = np.cos(phase)
    turn[:, KPAD : KPAD + KMAX + 1] = np.sin(phase)
    return project, rebuild, turn


def kernel(
    off_hbm,
    frac_hbm,
    cut_hbm,
    keep_hbm,
    mix_hbm,
    light_hbm,
    tracers_ref,
    kz_hbm,
    turn_hbm,
    project_hbm,
    rebuild_hbm,
    loss_hbm,
    source_hbm,
    out_ref,
    off_ref,
    frac_ref,
    cut_ref,
    keep_ref,
    mix_ref,
    light_ref,
    kz_ref,
    turn_ref,
    project_ref,
    rebuild_ref,
    loss_ref,
    source_ref,
    inp,
    kbuf,
    glow,
    rot,
    dp,
    cp,
    got,
    circ,
    given,
    taken,
    rows,
    relay,
    back,
    in_sem,
    fs,
    fr,
    es,
    ss,
    er,
    ls,
    lr,
    rs,
    rr,
    os,
    bs,
    br,
    arg_sem,
):
    lon = lax.axis_index("lon")
    lat = lax.axis_index("lat")
    me = lon % PEERS
    base = lon - me
    other = {"lon": (lon + PEERS) % (2 * PEERS), "lat": lat}
    has_south = lat > 0
    has_north = lat < 7
    plain_south = has_south & (lat != 4)
    plain_north = has_north & (lat != 3)

    def peer(p):
        return {"lon": base + p, "lat": lat}

    def tile_in(j):
        return pltpu.make_async_copy(
            tracers_ref.at[:, pl.ds(pl.multiple_of(j * 8, 8), 8), :], inp.at[j], in_sem.at[j]
        )

    def forth(j, src, dst, to):
        return pltpu.make_async_remote_copy(
            dp.at[j, src], got.at[j, dst], fs, fr.at[j], device_id=peer(to), device_id_type=MESH
        )

    def home(j, src, dst, to):
        return pltpu.make_async_remote_copy(
            got.at[j, src], back.at[j, dst], bs, br.at[j], device_id=peer(to), device_id_type=MESH
        )

    def edge_copy(j, n):
        return pltpu.make_async_remote_copy(
            given.at[j, pl.ds(EDGE - n, n)], taken.at[j, pl.ds(EDGE - n, n)], es, er.at[j],
            device_id=other, device_id_type=MESH,
        )

    def spec_copy(j, first, count):
        part = pl.ds(EDGE + first, count)
        return pltpu.make_async_remote_copy(
            given.at[j, part], taken.at[j, part], ss, er.at[j],
            device_id=other, device_id_type=MESH,
        )

    def in_class(lo, hi):
        return (lat >= lo) & (lat <= hi)

    def half(h):
        return pl.ds(h * DIRECT, DIRECT)

    def row_copy(j, h, slot, to):
        return pltpu.make_async_remote_copy(
            rows.at[2, j, half(h)], rows.at[slot, j, half(h)], ls.at[slot], lr.at[slot, h, j],
            device_id={"lon": lon, "lat": to}, device_id_type=MESH,
        )

    def relay_copy(j, to):
        return pltpu.make_async_remote_copy(
            rows.at[2, j, half(1)], relay.at[j], rs, rr.at[j],
            device_id={"lon": lon, "lat": to}, device_id_type=MESH,
        )

    def onward_copy(j, slot, to):
        return pltpu.make_async_remote_copy(
            relay.at[j], rows.at[slot, j, half(1)], os, lr.at[slot, 1, j],
            device_id={"lon": lon, "lat": to}, device_id_type=MESH,
        )

    def start_in(j, carry):
        tile_in(j).start()
        return carry

    pairs = (
        (kz_hbm, kz_ref),
        (off_hbm, off_ref),
        (frac_hbm, frac_ref),
        (cut_hbm, cut_ref),
        (keep_hbm, keep_ref),
        (mix_hbm, mix_ref),
        (light_hbm, light_ref),
        (turn_hbm, turn_ref),
        (project_hbm, project_ref),
        (rebuild_hbm, rebuild_ref),
        (loss_hbm, loss_ref),
        (source_hbm, source_ref),
    )
    arrivals = [
        pltpu.make_async_copy(src, dst, arg_sem.at[n]) for n, (src, dst) in enumerate(pairs)
    ]
    arrivals[0].start()
    lax.fori_loop(0, TILES, start_in, 0)
    for copy in arrivals[1:]:
        copy.start()

    @pl.when(lat == 7)
    def _():
        for first, last in ((LOW, KPAD), (KPAD + LOW, 2 * KPAD)):
            taken[:, EDGE + first : EDGE + last, :] = jnp.zeros((TILES, last - first, 128), jnp.float32)

    barrier = pltpu.get_barrier_semaphore()
    for d in range(1, PEERS):
        pl.semaphore_signal(barrier, inc=1, device_id=peer((me + d) % PEERS), device_id_type=MESH)
    pl.semaphore_signal(barrier, inc=1, device_id=other, device_id_type=MESH)

    @pl.when(has_south)
    def _():
        pl.semaphore_signal(
            barrier, inc=1, device_id={"lon": lon, "lat": lat - 1}, device_id_type=MESH
        )

    @pl.when(has_north)
    def _():
        pl.semaphore_signal(
            barrier, inc=1, device_id={"lon": lon, "lat": lat + 1}, device_id_type=MESH
        )

    for here, there in RELAYED:

        @pl.when(lat == here)
        def _():
            pl.semaphore_signal(
                barrier, inc=1, device_id={"lon": lon, "lat": there}, device_id_type=MESH
            )

    arrivals[0].wait()
    rot[...] = jnp.zeros_like(rot)
    rot[0:72, 0:CELLS] = kz_ref[...]
    kbuf[...] = rot[...].T[0:CELLS, :]

    def down(j, carry):
        last, e, kc = carry
        tile_in(j).wait()
        flat = inp.at[j].reshape(CELLS * 8, 128)
        kr = pltpu.roll(kbuf[...], lax.rem(128 - 8 * j, 128), 1)
        for p in range(8):
            kn = jnp.broadcast_to(kr[:, p + 1 : p + 2], (CELLS, 128))
            g = 1.0 + kc * e
            inv = 1.0 / (g + kn)
            last = (flat[pl.ds(p, CELLS, stride=8), :] + kc * last) * inv
            e = g * inv
            dp[j, p] = last
            cp[j, p] = kn * inv
            kc = kn
        return last, e, kc

    zero = jnp.zeros((CELLS, 128), jnp.float32)
    lax.fori_loop(
        0, TILES, down, (zero, zero + 1.0, jnp.broadcast_to(kbuf[:, 0:1], (CELLS, 128)))
    )

    edge_row = (lat == 0) | (lat == 7)
    cross_row = (lat == 3) | (lat == 4)

    @pl.when(edge_row)
    def _():
        pl.semaphore_wait(barrier, PEERS + 3)

    @pl.when(cross_row)
    def _():
        pl.semaphore_wait(barrier, PEERS + 4)

    @pl.when(jnp.logical_not(edge_row | cross_row))
    def _():
        pl.semaphore_wait(barrier, PEERS + 2)

    def up(c, x):
        j = TILES - 1 - c
        for p in reversed(range(8)):
            x = dp[j, p] + cp[j, p] * x
            dp[j, p] = x

        @pl.when(c == 0)
        def _():
            send(j)

        return x

    def send(j):
        for d in range(1, PEERS):
            to = (me + d) % PEERS
            forth(j, to, me, to).start()
        pltpu.make_async_copy(dp.at[j, me], got.at[j, me], fr.at[j]).start()

    lax.fori_loop(0, TILES, up, zero)

    for copy in arrivals[1:]:
        copy.wait()
    off = off_ref[0]
    frac = frac_ref[0]
    keep = keep_ref[0]
    mix = mix_ref[0]

    def light_row(c, carry):
        glow[pl.ds(c, 1), :] = jnp.full((1, 128), light_ref[0, c], jnp.float32)
        return carry

    lax.fori_loop(0, CELLS, light_row, 0)

    lane = lax.broadcasted_iota(jnp.int32, (1, 128), 1)
    wave = lane % KPAD
    share = jnp.where(wave <= cut_ref[0], jnp.where(wave == 0, 1.0, 2.0) / NLON, 0.0) * (1.0 - keep)
    turn = (1.0 - frac) * turn_ref[pl.ds(EDGE + off, 1), :] + frac * turn_ref[pl.ds(EDGE + 1 + off, 1), :]
    rot[...] = jnp.broadcast_to(turn * share, (128, 128)).T

    def gather(j):
        pltpu.make_async_copy(dp.at[j], got.at[j], fr.at[j]).wait()

        @pl.when(j == TILES - 1)
        def _():
            send(j - 1)

        @pl.when(j >= 2)
        def _():
            send(j - 2)

        for s in range(PEERS):
            circ[j, LEFT + CELLS * s : LEFT + CELLS * (s + 1), :] = got[j, s]
        for lo, hi, n, parts in CLASSES:

            @pl.when(in_class(lo, hi))
            def _():
                begin = jnp.clip(LEFT + (off + 1) * HALF, LEFT, RIGHT - n)
                given[j, EDGE - n : EDGE, :] = circ[j, pl.ds(begin, n), :]
                edge_copy(j, n).start()

        field = circ[j, LEFT:RIGHT, :]
        high = field.astype(jnp.bfloat16)
        low = (field - high.astype(jnp.float32)).astype(jnp.bfloat16)
        part = jnp.dot(
            project_ref[...], jnp.concatenate([high, low], axis=1), preferred_element_type=jnp.float32
        )
        n = 2 * KPAD
        given[j, EDGE : EDGE + n, :] = part[:n, :128] + part[n:, :128] + part[:n, 128:]
        for lo, hi, n, parts in CLASSES:

            @pl.when(in_class(lo, hi))
            def _():
                for first, count in parts:
                    spec_copy(j, first, count).start()

    def filt(j):
        for lo, hi, n, parts in CLASSES:

            @pl.when(in_class(lo, hi))
            def _():
                come = pl.ds(0, n + sum(count for _, count in parts))
                pltpu.make_async_copy(given.at[j, come], taken.at[j, come], er.at[j]).wait()
                fresh = taken[j, EDGE - n : EDGE, :]
                circ[j, LEFT - n : LEFT, :] = fresh
                circ[j, RIGHT : RIGHT + n, :] = fresh

        level = lax.broadcasted_iota(jnp.int32, (KPAD, 128), 0)
        sign = jnp.where(level % 2 == 0, 1.0, -1.0)
        cosine, sine = slice(EDGE, EDGE + KPAD), slice(EDGE + KPAD, EDGE + 2 * KPAD)
        a = given[j, cosine, :] + sign * taken[j, cosine, :]
        b = given[j, sine, :] + sign * taken[j, sine, :]
        c = rot[0:KPAD, :]
        d = rot[KPAD : 2 * KPAD, :]
        turned = jnp.concatenate([c * a - d * b, d * a + c * b], axis=0)
        high = turned.astype(jnp.bfloat16)
        low = (turned - high.astype(jnp.float32)).astype(jnp.bfloat16)
        weight = jnp.concatenate(
            [
                jnp.concatenate([high, low], axis=1),
                jnp.concatenate([high, jnp.zeros_like(low)], axis=1),
            ],
            axis=0,
        )
        for h in range(2):
            first = h * DIRECT
            lowpass = jnp.dot(
                rebuild_ref[first : first + DIRECT, :], weight, preferred_element_type=jnp.float32
            )
            near = circ[j, pl.ds(LEFT + first - off, DIRECT), :]
            far = circ[j, pl.ds(LEFT + first - 1 - off, DIRECT), :]
            moved = (1.0 - frac) * near + frac * far
            rows[2, j, first : first + DIRECT, :] = keep * moved + lowpass[:, :128] + lowpass[:, 128:]

            @pl.when(plain_north)
            def _():
                row_copy(j, h, 0, lat + 1).start()

            @pl.when(plain_south)
            def _():
                row_copy(j, h, 1, lat - 1).start()

            @pl.when(lat == 3)
            def _():
                (relay_copy(j, 7) if h else row_copy(j, 0, 0, 4)).start()

            @pl.when(lat == 4)
            def _():
                (relay_copy(j, 0) if h else row_copy(j, 0, 1, 3)).start()

    def onward(j):
        @pl.when(lat == 7)
        def _():
            relay_copy(j, 7).wait_recv()
            onward_copy(j, 0, 4).start()

        @pl.when(lat == 0)
        def _():
            relay_copy(j, 0).wait_recv()
            onward_copy(j, 1, 3).start()

    south_slot = jnp.where(has_south, 0, 2)
    north_slot = jnp.where(has_north, 1, 2)

    def spread(j):
        for h in range(2):

            @pl.when(has_south)
            def _():
                row_copy(j, h, 0, lat - 1).wait_recv()

            @pl.when(has_north)
            def _():
                row_copy(j, h, 1, lat + 1).wait_recv()

            for s in range(h * GROUP, (h + 1) * GROUP):
                part = pl.ds(CELLS * s, CELLS)
                got[j, s] = (1.0 - 2.0 * mix) * rows[2, j, part, :] + mix * (
                    rows[south_slot, j, part, :] + rows[north_slot, j, part, :]
                )
            for d in range(1, GROUP):
                to = h * GROUP + (me + d) % GROUP
                home(j, to, me, to).start()

            @pl.when(me // GROUP == h)
            def _():
                pltpu.make_async_copy(got.at[j, me], back.at[j, me], br.at[j]).start()

            @pl.when(me // GROUP != h)
            def _():
                to = h * GROUP + me % GROUP
                home(j, to, me, to).start()

    def finish(j):
        pltpu.make_async_copy(got.at[j], back.at[j], br.at[j]).wait()
        flat = out_ref.reshape(CELLS * LEVELS, 128)
        light = glow[...]
        for p in range(PEERS):
            level = j * 8 + p
            top = back[j, p] + source_ref[pl.ds(level, 1), :] * light
            flat[pl.ds(level, CELLS, stride=LEVELS), :] = top / (
                1.0 + loss_ref[pl.ds(level, 1), :] * light
            )

    stages = ((filt, 2), (gather, 0), (onward, 2), (finish, 4), (spread, 3))

    def step(t, carry):
        for stage, lag in stages:

            @pl.when((t >= lag) & (t < lag + TILES))
            def _():
                stage(TILES - 1 - (t - lag))

        return carry

    lax.fori_loop(0, TILES + 4, step, 0)

    sent = pl.ds(0, PEERS - 1)
    pltpu.make_async_copy(dp.at[:, sent], dp.at[:, sent], fs).wait()
    pltpu.make_async_copy(got.at[:, sent], got.at[:, sent], bs).wait()
    for lo, hi, n, parts in CLASSES:

        @pl.when(in_class(lo, hi))
        def _():
            edges = given.at[:, pl.ds(0, n)]
            spectra = given.at[:, pl.ds(0, sum(count for _, count in parts))]
            pltpu.make_async_copy(edges, edges, es).wait()
            pltpu.make_async_copy(spectra, spectra, ss).wait()

    whole, part = rows.at[2], rows.at[2, :, half(0)]

    @pl.when(plain_north)
    def _():
        pltpu.make_async_copy(whole, whole, ls.at[0]).wait()

    @pl.when(plain_south)
    def _():
        pltpu.make_async_copy(whole, whole, ls.at[1]).wait()

    @pl.when(lat == 3)
    def _():
        pltpu.make_async_copy(part, part, ls.at[0]).wait()

    @pl.when(lat == 4)
    def _():
        pltpu.make_async_copy(part, part, ls.at[1]).wait()

    @pl.when(cross_row)
    def _():
        pltpu.make_async_copy(relay, relay, rs).wait()

    @pl.when(edge_row)
    def _():
        pltpu.make_async_copy(relay, relay, os).wait()


def body(tracers, offsets, fraction, cutoffs, keep_high, mixing, kz, light, loss_rate, source):
    project, rebuild, turn = wave_tables()
    levels, species = tracers.shape[2:]
    hbm = pl.BlockSpec(memory_space=pltpu.HBM)
    f32 = jnp.float32
    dma = pltpu.SemaphoreType.DMA
    operands = (
        offsets,
        fraction,
        cutoffs,
        keep_high,
        mixing,
        light,
        tracers.reshape(CELLS, levels, species),
        kz.reshape(CELLS, levels).T,
        jnp.asarray(turn),
        jnp.asarray(project),
        jnp.asarray(rebuild),
        loss_rate,
        source,
    )
    out = pl.pallas_call(
        kernel,
        out_shape=pltpu.VMEM((CELLS, levels, species), f32),
        in_specs=[hbm] * 13,
        out_specs=pl.BlockSpec(memory_space=pltpu.VMEM),
        scratch_shapes=[
            pltpu.SMEM((1,), jnp.int32),
            pltpu.SMEM((1,), f32),
            pltpu.SMEM((1,), jnp.int32),
            pltpu.SMEM((1,), f32),
            pltpu.SMEM((1,), f32),
            pltpu.SMEM((1, CELLS), f32),
            pltpu.VMEM((levels, CELLS), f32),
            pltpu.VMEM(turn.shape, f32),
            pltpu.VMEM(project.shape, jnp.bfloat16),
            pltpu.VMEM(rebuild.shape, jnp.bfloat16),
            pltpu.VMEM((levels, species), f32),
            pltpu.VMEM((levels, species), f32),
            pltpu.VMEM((TILES, CELLS, 8, 128), f32),
            pltpu.VMEM((CELLS, 128), f32),
            pltpu.VMEM((CELLS, 128), f32),
            pltpu.VMEM((128, 128), f32),
            pltpu.VMEM((TILES, PEERS, CELLS, 128), f32),
            pltpu.VMEM((TILES, PEERS, CELLS, 128), f32),
            pltpu.VMEM((TILES, PEERS, CELLS, 128), f32),
            pltpu.VMEM((TILES, HALF + 2 * EDGE, 128), f32),
            pltpu.VMEM((TILES, EDGE + 2 * KPAD, 128), f32),
            pltpu.VMEM((TILES, EDGE + 2 * KPAD, 128), f32),
            pltpu.VMEM((3, TILES, HALF, 128), f32),
            pltpu.VMEM((TILES, DIRECT, 128), f32),
            pltpu.VMEM((TILES, PEERS, CELLS, 128), f32),
            dma((TILES,)),
            dma,
            dma((TILES,)),
            dma,
            dma,
            dma((TILES,)),
            dma((2,)),
            dma((2, 2, TILES)),
            dma,
            dma((TILES,)),
            dma,
            dma,
            dma((TILES,)),
            dma((12,)),
        ],
        compiler_params=pltpu.CompilerParams(
            collective_id=0, has_side_effects=True, vmem_limit_bytes=46 << 20
        ),
        name="transport",
    )(*[pltpu.with_memory_space_constraint(x, pltpu.HBM) if x.size > 1 else x for x in operands])
    return out.reshape(tracers.shape)


def solution(mesh):
    return jax.shard_map(
        body,
        mesh=mesh,
        in_specs=(
            P("lat", "lon", None, None),
            P("lat"),
            P("lat"),
            P("lat"),
            P("lat"),
            P("lat"),
            P("lat", "lon", None),
            P("lat", "lon"),
            P(),
            P(),
        ),
        out_specs=P("lat", "lon", None, None),
        check_vma=False,
    )
```

```python
import functools
import math

import jax
import jax.numpy as jnp
import numpy as np
from jax import lax
from jax.experimental import pallas as pl
from jax.experimental.pallas import tpu as pltpu
from jax.sharding import PartitionSpec as P

NLON = 1440
KMAX = 48
MESH = pl.DeviceIdType.MESH
CELLS = 90
PEERS = 8
HALF = CELLS * PEERS
LEVELS = 72
TILES = 9
EDGE = 184
KPAD = 56
DIRECT = HALF // 2
GROUP = PEERS // 2
RELAYED = ((3, 7), (7, 3), (7, 4), (4, 7), (4, 0), (0, 4), (0, 3), (3, 0))
LOW = 8
FULL = ((0, 2 * KPAD),)
CLASSES = (
    (0, 0, 48, FULL),
    (1, 2, 96, FULL),
    (3, 4, 136, FULL),
    (5, 6, EDGE, FULL),
    (7, 7, EDGE, ((0, LOW), (KPAD, LOW))),
)
LEFT = EDGE
RIGHT = EDGE + HALF


def split_bf16(table):
    import ml_dtypes

    high = table.astype(ml_dtypes.bfloat16)
    low = (table - high.astype(np.float64)).astype(ml_dtypes.bfloat16)
    return high, low


def wave_tables():
    places = np.arange(HALF)
    waves = np.arange(KMAX + 1)
    phase = (places[:, None] * waves[None, :] % NLON) * (2.0 * math.pi / NLON)
    table = np.zeros((HALF, 2 * KPAD))
    table[:, : KMAX + 1] = np.cos(phase)
    table[:, KPAD : KPAD + KMAX + 1] = np.sin(phase)
    high, low = split_bf16(table)
    rebuild = np.concatenate([high, low], axis=1)
    project = np.ascontiguousarray(rebuild.T)
    shifts = np.arange(-EDGE, EDGE)
    phase = (shifts[:, None] * waves[None, :] % NLON) * (2.0 * math.pi / NLON)
    turn = np.zeros((2 * EDGE, 128), np.float32)
    turn[:, : KMAX + 1] = np.cos(phase)
    turn[:, KPAD : KPAD + KMAX + 1] = np.sin(phase)
    return project, rebuild, turn


def kernel(
    off_hbm,
    frac_hbm,
    cut_hbm,
    keep_hbm,
    mix_hbm,
    light_hbm,
    tracers_ref,
    kz_hbm,
    turn_hbm,
    project_hbm,
    rebuild_hbm,
    loss_hbm,
    source_hbm,
    out_ref,
    off_ref,
    frac_ref,
    cut_ref,
    keep_ref,
    mix_ref,
    light_ref,
    kz_ref,
    turn_ref,
    project_ref,
    rebuild_ref,
    loss_ref,
    source_ref,
    inp,
    kbuf,
    glow,
    rot,
    dp,
    cp,
    got,
    circ,
    given,
    taken,
    rows,
    relay,
    back,
    in_sem,
    fs,
    fr,
    es,
    ss,
    er,
    ls,
    lr,
    rs,
    rr,
    os,
    bs,
    br,
    arg_sem,
):
    lon = lax.axis_index("lon")
    lat = lax.axis_index("lat")
    me = lon % PEERS
    base = lon - me
    other = {"lon": (lon + PEERS) % (2 * PEERS), "lat": lat}
    has_south = lat > 0
    has_north = lat < 7
    plain_south = has_south & (lat != 4)
    plain_north = has_north & (lat != 3)

    def peer(p):
        return {"lon": base + p, "lat": lat}

    def tile_in(j):
        return pltpu.make_async_copy(
            tracers_ref.at[:, pl.ds(pl.multiple_of(j * 8, 8), 8), :], inp.at[j], in_sem.at[j]
        )

    def forth(j, src, dst, to):
        return pltpu.make_async_remote_copy(
            dp.at[j, src], got.at[j, dst], fs, fr.at[j], device_id=peer(to), device_id_type=MESH
        )

    def home(j, src, dst, to):
        return pltpu.make_async_remote_copy(
            got.at[j, src], back.at[j, dst], bs, br.at[j], device_id=peer(to), device_id_type=MESH
        )

    def edge_copy(j, n):
        return pltpu.make_async_remote_copy(
            given.at[j, pl.ds(EDGE - n, n)], taken.at[j, pl.ds(EDGE - n, n)], es, er.at[j],
            device_id=other, device_id_type=MESH,
        )

    def spec_copy(j, first, count):
        part = pl.ds(EDGE + first, count)
        return pltpu.make_async_remote_copy(
            given.at[j, part], taken.at[j, part], ss, er.at[j],
            device_id=other, device_id_type=MESH,
        )

    def in_class(lo, hi):
        return (lat >= lo) & (lat <= hi)

    def half(h):
        return pl.ds(h * DIRECT, DIRECT)

    def row_copy(j, h, slot, to):
        return pltpu.make_async_remote_copy(
            rows.at[2, j, half(h)], rows.at[slot, j, half(h)], ls.at[slot], lr.at[slot, h, j],
            device_id={"lon": lon, "lat": to}, device_id_type=MESH,
        )

    def relay_copy(j, to):
        return pltpu.make_async_remote_copy(
            rows.at[2, j, half(1)], relay.at[j], rs, rr.at[j],
            device_id={"lon": lon, "lat": to}, device_id_type=MESH,
        )

    def onward_copy(j, slot, to):
        return pltpu.make_async_remote_copy(
            relay.at[j], rows.at[slot, j, half(1)], os, lr.at[slot, 1, j],
            device_id={"lon": lon, "lat": to}, device_id_type=MESH,
        )

    def start_in(j, carry):
        tile_in(j).start()
        return carry

    pairs = (
        (kz_hbm, kz_ref),
        (off_hbm, off_ref),
        (frac_hbm, frac_ref),
        (cut_hbm, cut_ref),
        (keep_hbm, keep_ref),
        (mix_hbm, mix_ref),
        (light_hbm, light_ref),
        (turn_hbm, turn_ref),
        (project_hbm, project_ref),
        (rebuild_hbm, rebuild_ref),
        (loss_hbm, loss_ref),
        (source_hbm, source_ref),
    )
    arrivals = [
        pltpu.make_async_copy(src, dst, arg_sem.at[n]) for n, (src, dst) in enumerate(pairs)
    ]
    arrivals[0].start()
    lax.fori_loop(0, TILES, start_in, 0)
    for copy in arrivals[1:]:
        copy.start()

    @pl.when(lat == 7)
    def _():
        for first, last in ((LOW, KPAD), (KPAD + LOW, 2 * KPAD)):
            taken[:, EDGE + first : EDGE + last, :] = jnp.zeros((TILES, last - first, 128), jnp.float32)

    barrier = pltpu.get_barrier_semaphore()
    for d in range(1, PEERS):
        pl.semaphore_signal(barrier, inc=1, device_id=peer((me + d) % PEERS), device_id_type=MESH)
    pl.semaphore_signal(barrier, inc=1, device_id=other, device_id_type=MESH)

    @pl.when(has_south)
    def _():
        pl.semaphore_signal(
            barrier, inc=1, device_id={"lon": lon, "lat": lat - 1}, device_id_type=MESH
        )

    @pl.when(has_north)
    def _():
        pl.semaphore_signal(
            barrier, inc=1, device_id={"lon": lon, "lat": lat + 1}, device_id_type=MESH
        )

    for here, there in RELAYED:

        @pl.when(lat == here)
        def _():
            pl.semaphore_signal(
                barrier, inc=1, device_id={"lon": lon, "lat": there}, device_id_type=MESH
            )

    arrivals[0].wait()
    rot[...] = jnp.zeros_like(rot)
    rot[0:72, 0:CELLS] = kz_ref[...]
    kbuf[...] = rot[...].T[0:CELLS, :]

    def down(j, carry):
        last, e, kc = carry
        tile_in(j).wait()
        flat = inp.at[j].reshape(CELLS * 8, 128)
        kr = pltpu.roll(kbuf[...], lax.rem(128 - 8 * j, 128), 1)
        for p in range(8):
            kn = jnp.broadcast_to(kr[:, p + 1 : p + 2], (CELLS, 128))
            g = 1.0 + kc * e
            inv = 1.0 / (g + kn)
            last = (flat[pl.ds(p, CELLS, stride=8), :] + kc * last) * inv
            e = g * inv
            dp[j, p] = last
            cp[j, p] = kn * inv
            kc = kn
        return last, e, kc

    zero = jnp.zeros((CELLS, 128), jnp.float32)
    lax.fori_loop(
        0, TILES, down, (zero, zero + 1.0, jnp.broadcast_to(kbuf[:, 0:1], (CELLS, 128)))
    )

    edge_row = (lat == 0) | (lat == 7)
    cross_row = (lat == 3) | (lat == 4)

    @pl.when(edge_row)
    def _():
        pl.semaphore_wait(barrier, PEERS + 3)

    @pl.when(cross_row)
    def _():
        pl.semaphore_wait(barrier, PEERS + 4)

    @pl.when(jnp.logical_not(edge_row | cross_row))
    def _():
        pl.semaphore_wait(barrier, PEERS + 2)

    def up(c, x):
        j = TILES - 1 - c
        for p in reversed(range(8)):
            x = dp[j, p] + cp[j, p] * x
            dp[j, p] = x

        @pl.when(c == 0)
        def _():
            send(j, 0)

        return x

    def send(j, core):
        for d in range(1, GROUP):
            to = (me // 2 + d) % GROUP * 2 + core
            forth(j, to, me, to).start()
        near = me // 2 * 2 + core

        @pl.when(near == me)
        def _():
            pltpu.make_async_copy(dp.at[j, me], got.at[j, me], fr.at[j]).start()

        @pl.when(near != me)
        def _():
            forth(j, near, me, near).start()

    lax.fori_loop(0, TILES, up, zero)

    for copy in arrivals[1:]:
        copy.wait()
    off = off_ref[0]
    frac = frac_ref[0]
    keep = keep_ref[0]
    mix = mix_ref[0]

    def light_row(c, carry):
        glow[pl.ds(c, 1), :] = jnp.full((1, 128), light_ref[0, c], jnp.float32)
        return carry

    lax.fori_loop(0, CELLS, light_row, 0)

    lane = lax.broadcasted_iota(jnp.int32, (1, 128), 1)
    wave = lane % KPAD
    share = jnp.where(wave <= cut_ref[0], jnp.where(wave == 0, 1.0, 2.0) / NLON, 0.0) * (1.0 - keep)
    turn = (1.0 - frac) * turn_ref[pl.ds(EDGE + off, 1), :] + frac * turn_ref[pl.ds(EDGE + 1 + off, 1), :]
    rot[...] = jnp.broadcast_to(turn * share, (128, 128)).T

    send(TILES - 1, 1)

    def gather(j):
        pltpu.make_async_copy(dp.at[j], got.at[j], fr.at[j]).wait()

        @pl.when(j == TILES - 1)
        def _():
            send(j - 1, 0)
            send(j - 1, 1)

        @pl.when(j >= 2)
        def _():
            send(j - 2, 0)
            send(j - 2, 1)

        for s in range(PEERS):
            circ[j, LEFT + CELLS * s : LEFT + CELLS * (s + 1), :] = got[j, s]
        for lo, hi, n, parts in CLASSES:

            @pl.when(in_class(lo, hi))
            def _():
                begin = jnp.clip(LEFT + (off + 1) * HALF, LEFT, RIGHT - n)
                given[j, EDGE - n : EDGE, :] = circ[j, pl.ds(begin, n), :]
                edge_copy(j, n).start()

        field = circ[j, LEFT:RIGHT, :]
        high = field.astype(jnp.bfloat16)
        low = (field - high.astype(jnp.float32)).astype(jnp.bfloat16)
        part = jnp.dot(
            project_ref[...], jnp.concatenate([high, low], axis=1), preferred_element_type=jnp.float32
        )
        n = 2 * KPAD
        given[j, EDGE : EDGE + n, :] = part[:n, :128] + part[n:, :128] + part[:n, 128:]
        for lo, hi, n, parts in CLASSES:

            @pl.when(in_class(lo, hi))
            def _():
                for first, count in parts:
                    spec_copy(j, first, count).start()

    def filt(j):
        for lo, hi, n, parts in CLASSES:

            @pl.when(in_class(lo, hi))
            def _():
                come = pl.ds(0, n + sum(count for _, count in parts))
                pltpu.make_async_copy(given.at[j, come], taken.at[j, come], er.at[j]).wait()
                fresh = taken[j, EDGE - n : EDGE, :]
                circ[j, LEFT - n : LEFT, :] = fresh
                circ[j, RIGHT : RIGHT + n, :] = fresh

        level = lax.broadcasted_iota(jnp.int32, (KPAD, 128), 0)
        sign = jnp.where(level % 2 == 0, 1.0, -1.0)
        cosine, sine = slice(EDGE, EDGE + KPAD), slice(EDGE + KPAD, EDGE + 2 * KPAD)
        a = given[j, cosine, :] + sign * taken[j, cosine, :]
        b = given[j, sine, :] + sign * taken[j, sine, :]
        c = rot[0:KPAD, :]
        d = rot[KPAD : 2 * KPAD, :]
        turned = jnp.concatenate([c * a - d * b, d * a + c * b], axis=0)
        high = turned.astype(jnp.bfloat16)
        low = (turned - high.astype(jnp.float32)).astype(jnp.bfloat16)
        weight = jnp.concatenate(
            [
                jnp.concatenate([high, low], axis=1),
                jnp.concatenate([high, jnp.zeros_like(low)], axis=1),
            ],
            axis=0,
        )
        for h in range(2):
            first = h * DIRECT
            lowpass = jnp.dot(
                rebuild_ref[first : first + DIRECT, :], weight, preferred_element_type=jnp.float32
            )
            near = circ[j, pl.ds(LEFT + first - off, DIRECT), :]
            far = circ[j, pl.ds(LEFT + first - 1 - off, DIRECT), :]
            moved = (1.0 - frac) * near + frac * far
            rows[2, j, first : first + DIRECT, :] = keep * moved + lowpass[:, :128] + lowpass[:, 128:]

            @pl.when(plain_north)
            def _():
                row_copy(j, h, 0, lat + 1).start()

            @pl.when(plain_south)
            def _():
                row_copy(j, h, 1, lat - 1).start()

            @pl.when(lat == 3)
            def _():
                (relay_copy(j, 7) if h else row_copy(j, 0, 0, 4)).start()

            @pl.when(lat == 4)
            def _():
                (relay_copy(j, 0) if h else row_copy(j, 0, 1, 3)).start()

    def onward(j):
        @pl.when(lat == 7)
        def _():
            relay_copy(j, 7).wait_recv()
            onward_copy(j, 0, 4).start()

        @pl.when(lat == 0)
        def _():
            relay_copy(j, 0).wait_recv()
            onward_copy(j, 1, 3).start()

    south_slot = jnp.where(has_south, 0, 2)
    north_slot = jnp.where(has_north, 1, 2)

    def spread(j):
        for h in range(2):

            @pl.when(has_south)
            def _():
                row_copy(j, h, 0, lat - 1).wait_recv()

            @pl.when(has_north)
            def _():
                row_copy(j, h, 1, lat + 1).wait_recv()

            for s in range(h * GROUP, (h + 1) * GROUP):
                part = pl.ds(CELLS * s, CELLS)
                got[j, s] = (1.0 - 2.0 * mix) * rows[2, j, part, :] + mix * (
                    rows[south_slot, j, part, :] + rows[north_slot, j, part, :]
                )
            for d in range(1, GROUP):
                to = h * GROUP + (me + d) % GROUP
                home(j, to, me, to).start()

            @pl.when(me // GROUP == h)
            def _():
                pltpu.make_async_copy(got.at[j, me], back.at[j, me], br.at[j]).start()

            @pl.when(me // GROUP != h)
            def _():
                to = h * GROUP + me % GROUP
                home(j, to, me, to).start()

    def finish(j):
        pltpu.make_async_copy(got.at[j], back.at[j], br.at[j]).wait()
        flat = out_ref.reshape(CELLS * LEVELS, 128)
        light = glow[...]
        for p in range(PEERS):
            level = j * 8 + p
            top = back[j, p] + source_ref[pl.ds(level, 1), :] * light
            flat[pl.ds(level, CELLS, stride=LEVELS), :] = top / (
                1.0 + loss_ref[pl.ds(level, 1), :] * light
            )

    stages = ((filt, 2), (gather, 0), (onward, 2), (finish, 4), (spread, 3))

    def step(t, carry):
        for stage, lag in stages:

            @pl.when((t >= lag) & (t < lag + TILES))
            def _():
                stage(TILES - 1 - (t - lag))

        return carry

    lax.fori_loop(0, TILES + 4, step, 0)

    sent = pl.ds(0, PEERS - 1)
    pltpu.make_async_copy(dp.at[:, sent], dp.at[:, sent], fs).wait()
    pltpu.make_async_copy(got.at[:, sent], got.at[:, sent], bs).wait()
    for lo, hi, n, parts in CLASSES:

        @pl.when(in_class(lo, hi))
        def _():
            edges = given.at[:, pl.ds(0, n)]
            spectra = given.at[:, pl.ds(0, sum(count for _, count in parts))]
            pltpu.make_async_copy(edges, edges, es).wait()
            pltpu.make_async_copy(spectra, spectra, ss).wait()

    whole, part = rows.at[2], rows.at[2, :, half(0)]

    @pl.when(plain_north)
    def _():
        pltpu.make_async_copy(whole, whole, ls.at[0]).wait()

    @pl.when(plain_south)
    def _():
        pltpu.make_async_copy(whole, whole, ls.at[1]).wait()

    @pl.when(lat == 3)
    def _():
        pltpu.make_async_copy(part, part, ls.at[0]).wait()

    @pl.when(lat == 4)
    def _():
        pltpu.make_async_copy(part, part, ls.at[1]).wait()

    @pl.when(cross_row)
    def _():
        pltpu.make_async_copy(relay, relay, rs).wait()

    @pl.when(edge_row)
    def _():
        pltpu.make_async_copy(relay, relay, os).wait()


def body(tracers, offsets, fraction, cutoffs, keep_high, mixing, kz, light, loss_rate, source):
    project, rebuild, turn = wave_tables()
    levels, species = tracers.shape[2:]
    hbm = pl.BlockSpec(memory_space=pltpu.HBM)
    f32 = jnp.float32
    dma = pltpu.SemaphoreType.DMA
    operands = (
        offsets,
        fraction,
        cutoffs,
        keep_high,
        mixing,
        light,
        tracers.reshape(CELLS, levels, species),
        kz.reshape(CELLS, levels).T,
        jnp.asarray(turn),
        jnp.asarray(project),
        jnp.asarray(rebuild),
        loss_rate,
        source,
    )
    out = pl.pallas_call(
        kernel,
        out_shape=pltpu.VMEM((CELLS, levels, species), f32),
        in_specs=[hbm] * 13,
        out_specs=pl.BlockSpec(memory_space=pltpu.VMEM),
        scratch_shapes=[
            pltpu.SMEM((1,), jnp.int32),
            pltpu.SMEM((1,), f32),
            pltpu.SMEM((1,), jnp.int32),
            pltpu.SMEM((1,), f32),
            pltpu.SMEM((1,), f32),
            pltpu.SMEM((1, CELLS), f32),
            pltpu.VMEM((levels, CELLS), f32),
            pltpu.VMEM(turn.shape, f32),
            pltpu.VMEM(project.shape, jnp.bfloat16),
            pltpu.VMEM(rebuild.shape, jnp.bfloat16),
            pltpu.VMEM((levels, species), f32),
            pltpu.VMEM((levels, species), f32),
            pltpu.VMEM((TILES, CELLS, 8, 128), f32),
            pltpu.VMEM((CELLS, 128), f32),
            pltpu.VMEM((CELLS, 128), f32),
            pltpu.VMEM((128, 128), f32),
            pltpu.VMEM((TILES, PEERS, CELLS, 128), f32),
            pltpu.VMEM((TILES, PEERS, CELLS, 128), f32),
            pltpu.VMEM((TILES, PEERS, CELLS, 128), f32),
            pltpu.VMEM((TILES, HALF + 2 * EDGE, 128), f32),
            pltpu.VMEM((TILES, EDGE + 2 * KPAD, 128), f32),
            pltpu.VMEM((TILES, EDGE + 2 * KPAD, 128), f32),
            pltpu.VMEM((3, TILES, HALF, 128), f32),
            pltpu.VMEM((TILES, DIRECT, 128), f32),
            pltpu.VMEM((TILES, PEERS, CELLS, 128), f32),
            dma((TILES,)),
            dma,
            dma((TILES,)),
            dma,
            dma,
            dma((TILES,)),
            dma((2,)),
            dma((2, 2, TILES)),
            dma,
            dma((TILES,)),
            dma,
            dma,
            dma((TILES,)),
            dma((12,)),
        ],
        compiler_params=pltpu.CompilerParams(
            collective_id=0, has_side_effects=True, vmem_limit_bytes=46 << 20
        ),
        name="transport",
    )(*[pltpu.with_memory_space_constraint(x, pltpu.HBM) if x.size > 1 else x for x in operands])
    return out.reshape(tracers.shape)


def solution(mesh):
    return jax.shard_map(
        body,
        mesh=mesh,
        in_specs=(
            P("lat", "lon", None, None),
            P("lat"),
            P("lat"),
            P("lat"),
            P("lat"),
            P("lat"),
            P("lat", "lon", None),
            P("lat", "lon"),
            P(),
            P(),
        ),
        out_specs=P("lat", "lon", None, None),
        check_vma=False,
    )
```

```python
import functools
import math

import jax
import jax.numpy as jnp
import numpy as np
from jax import lax
from jax.experimental import pallas as pl
from jax.experimental.pallas import tpu as pltpu
from jax.sharding import PartitionSpec as P

NLON = 1440
KMAX = 48
MESH = pl.DeviceIdType.MESH
CELLS = 90
PEERS = 8
HALF = CELLS * PEERS
LEVELS = 72
TILES = 9
EDGE = 184
KPAD = 56
DIRECT = HALF // 2
GROUP = PEERS // 2
RELAYED = ((3, 7), (7, 3), (7, 4), (4, 7), (4, 0), (0, 4), (0, 3), (3, 0))
LOW = 8
FULL = ((0, 2 * KPAD),)
CLASSES = (
    (0, 0, 48, FULL),
    (1, 2, 96, FULL),
    (3, 4, 136, FULL),
    (5, 6, EDGE, FULL),
    (7, 7, EDGE, ((0, LOW), (KPAD, LOW))),
)
LEFT = EDGE
RIGHT = EDGE + HALF


def split_bf16(table):
    import ml_dtypes

    high = table.astype(ml_dtypes.bfloat16)
    low = (table - high.astype(np.float64)).astype(ml_dtypes.bfloat16)
    return high, low


def wave_tables():
    places = np.arange(HALF)
    waves = np.arange(KMAX + 1)
    phase = (places[:, None] * waves[None, :] % NLON) * (2.0 * math.pi / NLON)
    table = np.zeros((HALF, 2 * KPAD))
    table[:, : KMAX + 1] = np.cos(phase)
    table[:, KPAD : KPAD + KMAX + 1] = np.sin(phase)
    high, low = split_bf16(table)
    rebuild = np.concatenate([high, low], axis=1)
    project = np.ascontiguousarray(rebuild.T)
    shifts = np.arange(-EDGE, EDGE)
    phase = (shifts[:, None] * waves[None, :] % NLON) * (2.0 * math.pi / NLON)
    turn = np.zeros((2 * EDGE, 128), np.float32)
    turn[:, : KMAX + 1] = np.cos(phase)
    turn[:, KPAD : KPAD + KMAX + 1] = np.sin(phase)
    return project, rebuild, turn


def kernel(
    off_hbm,
    frac_hbm,
    cut_hbm,
    keep_hbm,
    mix_hbm,
    light_hbm,
    tracers_ref,
    kz_hbm,
    turn_hbm,
    project_hbm,
    rebuild_hbm,
    loss_hbm,
    source_hbm,
    out_ref,
    off_ref,
    frac_ref,
    cut_ref,
    keep_ref,
    mix_ref,
    light_ref,
    kz_ref,
    turn_ref,
    project_ref,
    rebuild_ref,
    loss_ref,
    source_ref,
    inp,
    kbuf,
    glow,
    rot,
    dp,
    cp,
    got,
    circ,
    given,
    taken,
    rows,
    relay,
    back,
    in_sem,
    fs,
    fr,
    es,
    ss,
    er,
    ls,
    lr,
    rs,
    rr,
    os,
    bs,
    br,
    arg_sem,
):
    lon = lax.axis_index("lon")
    lat = lax.axis_index("lat")
    me = lon % PEERS
    base = lon - me
    other = {"lon": (lon + PEERS) % (2 * PEERS), "lat": lat}
    has_south = lat > 0
    has_north = lat < 7
    plain_south = has_south & (lat != 4)
    plain_north = has_north & (lat != 3)

    def peer(p):
        return {"lon": base + p, "lat": lat}

    def tile_in(j):
        return pltpu.make_async_copy(
            tracers_ref.at[:, pl.ds(pl.multiple_of(j * 8, 8), 8), :], inp.at[j], in_sem.at[j]
        )

    def forth(j, src, dst, to):
        return pltpu.make_async_remote_copy(
            dp.at[j, src], got.at[j, dst], fs, fr.at[j], device_id=peer(to), device_id_type=MESH
        )

    def home(j, src, dst, to):
        return pltpu.make_async_remote_copy(
            got.at[j, src], back.at[j, dst], bs, br.at[j], device_id=peer(to), device_id_type=MESH
        )

    def edge_copy(j, n):
        return pltpu.make_async_remote_copy(
            given.at[j, pl.ds(EDGE - n, n)], taken.at[j, pl.ds(EDGE - n, n)], es, er.at[j],
            device_id=other, device_id_type=MESH,
        )

    def spec_copy(j, first, count):
        part = pl.ds(EDGE + first, count)
        return pltpu.make_async_remote_copy(
            given.at[j, part], taken.at[j, part], ss, er.at[j],
            device_id=other, device_id_type=MESH,
        )

    def in_class(lo, hi):
        return (lat >= lo) & (lat <= hi)

    def half(h):
        return pl.ds(h * DIRECT, DIRECT)

    def row_copy(j, h, slot, to):
        return pltpu.make_async_remote_copy(
            rows.at[2, j, half(h)], rows.at[slot, j, half(h)], ls.at[slot], lr.at[slot, h, j],
            device_id={"lon": lon, "lat": to}, device_id_type=MESH,
        )

    def relay_copy(j, to):
        return pltpu.make_async_remote_copy(
            rows.at[2, j, half(1)], relay.at[j], rs, rr.at[j],
            device_id={"lon": lon, "lat": to}, device_id_type=MESH,
        )

    def onward_copy(j, slot, to):
        return pltpu.make_async_remote_copy(
            relay.at[j], rows.at[slot, j, half(1)], os, lr.at[slot, 1, j],
            device_id={"lon": lon, "lat": to}, device_id_type=MESH,
        )

    def start_in(j, carry):
        tile_in(j).start()
        return carry

    pairs = (
        (kz_hbm, kz_ref),
        (off_hbm, off_ref),
        (frac_hbm, frac_ref),
        (cut_hbm, cut_ref),
        (keep_hbm, keep_ref),
        (mix_hbm, mix_ref),
        (light_hbm, light_ref),
        (turn_hbm, turn_ref),
        (project_hbm, project_ref),
        (rebuild_hbm, rebuild_ref),
        (loss_hbm, loss_ref),
        (source_hbm, source_ref),
    )
    arrivals = [
        pltpu.make_async_copy(src, dst, arg_sem.at[n]) for n, (src, dst) in enumerate(pairs)
    ]
    arrivals[0].start()
    lax.fori_loop(0, TILES, start_in, 0)
    for copy in arrivals[1:]:
        copy.start()

    @pl.when(lat == 7)
    def _():
        for first, last in ((LOW, KPAD), (KPAD + LOW, 2 * KPAD)):
            taken[:, EDGE + first : EDGE + last, :] = jnp.zeros((TILES, last - first, 128), jnp.float32)

    barrier = pltpu.get_barrier_semaphore()
    for d in range(1, PEERS):
        pl.semaphore_signal(barrier, inc=1, device_id=peer((me + d) % PEERS), device_id_type=MESH)
    pl.semaphore_signal(barrier, inc=1, device_id=other, device_id_type=MESH)

    @pl.when(has_south)
    def _():
        pl.semaphore_signal(
            barrier, inc=1, device_id={"lon": lon, "lat": lat - 1}, device_id_type=MESH
        )

    @pl.when(has_north)
    def _():
        pl.semaphore_signal(
            barrier, inc=1, device_id={"lon": lon, "lat": lat + 1}, device_id_type=MESH
        )

    for here, there in RELAYED:

        @pl.when(lat == here)
        def _():
            pl.semaphore_signal(
                barrier, inc=1, device_id={"lon": lon, "lat": there}, device_id_type=MESH
            )

    arrivals[0].wait()
    rot[...] = jnp.zeros_like(rot)
    rot[0:72, 0:CELLS] = kz_ref[...]
    kbuf[...] = rot[...].T[0:CELLS, :]

    def down(j, carry):
        last, e, kc = carry
        tile_in(j).wait()
        flat = inp.at[j].reshape(CELLS * 8, 128)
        kr = pltpu.roll(kbuf[...], lax.rem(128 - 8 * j, 128), 1)
        for p in range(8):
            kn = jnp.broadcast_to(kr[:, p + 1 : p + 2], (CELLS, 128))
            g = 1.0 + kc * e
            inv = 1.0 / (g + kn)
            last = (flat[pl.ds(p, CELLS, stride=8), :] + kc * last) * inv
            e = g * inv
            dp[j, p] = last
            cp[j, p] = kn * inv
            kc = kn
        return last, e, kc

    zero = jnp.zeros((CELLS, 128), jnp.float32)
    lax.fori_loop(
        0, TILES, down, (zero, zero + 1.0, jnp.broadcast_to(kbuf[:, 0:1], (CELLS, 128)))
    )

    edge_row = (lat == 0) | (lat == 7)
    cross_row = (lat == 3) | (lat == 4)

    @pl.when(edge_row)
    def _():
        pl.semaphore_wait(barrier, PEERS + 3)

    @pl.when(cross_row)
    def _():
        pl.semaphore_wait(barrier, PEERS + 4)

    @pl.when(jnp.logical_not(edge_row | cross_row))
    def _():
        pl.semaphore_wait(barrier, PEERS + 2)

    def up(c, x):
        j = TILES - 1 - c
        for p in reversed(range(8)):
            x = dp[j, p] + cp[j, p] * x
            dp[j, p] = x

        @pl.when(c == 0)
        def _():
            send(j, 0)

        return x

    def send(j, core):
        for d in range(1, GROUP):
            to = (me // 2 + d) % GROUP * 2 + core
            forth(j, to, me, to).start()
        near = me // 2 * 2 + core

        @pl.when(near == me)
        def _():
            pltpu.make_async_copy(dp.at[j, me], got.at[j, me], fr.at[j]).start()

        @pl.when(near != me)
        def _():
            forth(j, near, me, near).start()

    lax.fori_loop(0, TILES, up, zero)

    for copy in arrivals[1:]:
        copy.wait()
    off = off_ref[0]
    frac = frac_ref[0]
    keep = keep_ref[0]
    mix = mix_ref[0]

    def light_row(c, carry):
        glow[pl.ds(c, 1), :] = jnp.full((1, 128), light_ref[0, c], jnp.float32)
        return carry

    lax.fori_loop(0, CELLS, light_row, 0)

    lane = lax.broadcasted_iota(jnp.int32, (1, 128), 1)
    wave = lane % KPAD
    share = jnp.where(wave <= cut_ref[0], jnp.where(wave == 0, 1.0, 2.0) / NLON, 0.0) * (1.0 - keep)
    turn = (1.0 - frac) * turn_ref[pl.ds(EDGE + off, 1), :] + frac * turn_ref[pl.ds(EDGE + 1 + off, 1), :]
    rot[...] = jnp.broadcast_to(turn * share, (128, 128)).T

    send(TILES - 1, 1)

    def gather(j):
        pltpu.make_async_copy(dp.at[j], got.at[j], fr.at[j]).wait()

        @pl.when(j == TILES - 1)
        def _():
            send(j - 1, 0)
            send(j - 1, 1)

        @pl.when(j >= 2)
        def _():
            send(j - 2, 0)
            send(j - 2, 1)

        for s in range(PEERS):
            circ[j, LEFT + CELLS * s : LEFT + CELLS * (s + 1), :] = got[j, s]
        for lo, hi, n, parts in CLASSES:

            @pl.when(in_class(lo, hi))
            def _():
                begin = jnp.clip(LEFT + (off + 1) * HALF, LEFT, RIGHT - n)
                given[j, EDGE - n : EDGE, :] = circ[j, pl.ds(begin, n), :]
                edge_copy(j, n).start()

        field = circ[j, LEFT:RIGHT, :]
        high = field.astype(jnp.bfloat16)
        low = (field - high.astype(jnp.float32)).astype(jnp.bfloat16)
        part = jnp.dot(
            project_ref[...], jnp.concatenate([high, low], axis=1), preferred_element_type=jnp.float32
        )
        n = 2 * KPAD
        given[j, EDGE : EDGE + n, :] = part[:n, :128] + part[n:, :128] + part[:n, 128:]
        for lo, hi, n, parts in CLASSES:

            @pl.when(in_class(lo, hi))
            def _():
                for first, count in parts:
                    spec_copy(j, first, count).start()

    def filt(j):
        for lo, hi, n, parts in CLASSES:

            @pl.when(in_class(lo, hi))
            def _():
                come = pl.ds(0, n + sum(count for _, count in parts))
                pltpu.make_async_copy(given.at[j, come], taken.at[j, come], er.at[j]).wait()
                fresh = taken[j, EDGE - n : EDGE, :]
                circ[j, LEFT - n : LEFT, :] = fresh
                circ[j, RIGHT : RIGHT + n, :] = fresh

        level = lax.broadcasted_iota(jnp.int32, (KPAD, 128), 0)
        sign = jnp.where(level % 2 == 0, 1.0, -1.0)
        cosine, sine = slice(EDGE, EDGE + KPAD), slice(EDGE + KPAD, EDGE + 2 * KPAD)
        a = given[j, cosine, :] + sign * taken[j, cosine, :]
        b = given[j, sine, :] + sign * taken[j, sine, :]
        c = rot[0:KPAD, :]
        d = rot[KPAD : 2 * KPAD, :]
        turned = jnp.concatenate([c * a - d * b, d * a + c * b], axis=0)
        high = turned.astype(jnp.bfloat16)
        low = (turned - high.astype(jnp.float32)).astype(jnp.bfloat16)
        weight = jnp.concatenate(
            [
                jnp.concatenate([high, low], axis=1),
                jnp.concatenate([high, jnp.zeros_like(low)], axis=1),
            ],
            axis=0,
        )
        for h in range(2):
            first = h * DIRECT
            lowpass = jnp.dot(
                rebuild_ref[first : first + DIRECT, :], weight, preferred_element_type=jnp.float32
            )
            near = circ[j, pl.ds(LEFT + first - off, DIRECT), :]
            far = circ[j, pl.ds(LEFT + first - 1 - off, DIRECT), :]
            moved = (1.0 - frac) * near + frac * far
            rows[2, j, first : first + DIRECT, :] = keep * moved + lowpass[:, :128] + lowpass[:, 128:]

            @pl.when(plain_north)
            def _():
                row_copy(j, h, 0, lat + 1).start()

            @pl.when(plain_south)
            def _():
                row_copy(j, h, 1, lat - 1).start()

            @pl.when(lat == 3)
            def _():
                (relay_copy(j, 7) if h else row_copy(j, 0, 0, 4)).start()

            @pl.when(lat == 4)
            def _():
                (relay_copy(j, 0) if h else row_copy(j, 0, 1, 3)).start()

    def onward(j):
        @pl.when(lat == 7)
        def _():
            relay_copy(j, 7).wait_recv()
            onward_copy(j, 0, 4).start()

        @pl.when(lat == 0)
        def _():
            relay_copy(j, 0).wait_recv()
            onward_copy(j, 1, 3).start()

    south_slot = jnp.where(has_south, 0, 2)
    north_slot = jnp.where(has_north, 1, 2)

    def spread(j):
        for h in range(2):

            @pl.when(has_south)
            def _():
                row_copy(j, h, 0, lat - 1).wait_recv()

            @pl.when(has_north)
            def _():
                row_copy(j, h, 1, lat + 1).wait_recv()

            for s in range(h * GROUP, (h + 1) * GROUP):
                part = pl.ds(CELLS * s, CELLS)
                got[j, s] = (1.0 - 2.0 * mix) * rows[2, j, part, :] + mix * (
                    rows[south_slot, j, part, :] + rows[north_slot, j, part, :]
                )
            for d in range(1, GROUP):
                to = h * GROUP + (me + d) % GROUP
                home(j, to, me, to).start()

            @pl.when(me // GROUP == h)
            def _():
                pltpu.make_async_copy(got.at[j, me], back.at[j, me], br.at[j]).start()

            @pl.when(me // GROUP != h)
            def _():
                to = h * GROUP + me % GROUP
                home(j, to, me, to).start()

    def finish(j):
        pltpu.make_async_copy(got.at[j], back.at[j], br.at[j]).wait()
        flat = out_ref.reshape(CELLS * LEVELS, 128)
        light = glow[...]
        for p in range(PEERS):
            level = j * 8 + p
            top = back[j, p] + source_ref[pl.ds(level, 1), :] * light
            flat[pl.ds(level, CELLS, stride=LEVELS), :] = top / (
                1.0 + loss_ref[pl.ds(level, 1), :] * light
            )

    stages = ((filt, 2), (gather, 0), (onward, 2), (spread, 3), (finish, 5))

    def step(t, carry):
        @pl.when(t == 1)
        def _():
            filt(TILES - 1)

        for stage, lag in stages:

            @pl.when((t >= lag + (stage is filt)) & (t < lag + TILES))
            def _():
                stage(TILES - 1 - (t - lag))

        return carry

    lax.fori_loop(0, TILES + 5, step, 0)

    sent = pl.ds(0, PEERS - 1)
    pltpu.make_async_copy(dp.at[:, sent], dp.at[:, sent], fs).wait()
    pltpu.make_async_copy(got.at[:, sent], got.at[:, sent], bs).wait()
    for lo, hi, n, parts in CLASSES:

        @pl.when(in_class(lo, hi))
        def _():
            edges = given.at[:, pl.ds(0, n)]
            spectra = given.at[:, pl.ds(0, sum(count for _, count in parts))]
            pltpu.make_async_copy(edges, edges, es).wait()
            pltpu.make_async_copy(spectra, spectra, ss).wait()

    whole, part = rows.at[2], rows.at[2, :, half(0)]

    @pl.when(plain_north)
    def _():
        pltpu.make_async_copy(whole, whole, ls.at[0]).wait()

    @pl.when(plain_south)
    def _():
        pltpu.make_async_copy(whole, whole, ls.at[1]).wait()

    @pl.when(lat == 3)
    def _():
        pltpu.make_async_copy(part, part, ls.at[0]).wait()

    @pl.when(lat == 4)
    def _():
        pltpu.make_async_copy(part, part, ls.at[1]).wait()

    @pl.when(cross_row)
    def _():
        pltpu.make_async_copy(relay, relay, rs).wait()

    @pl.when(edge_row)
    def _():
        pltpu.make_async_copy(relay, relay, os).wait()


def body(tracers, offsets, fraction, cutoffs, keep_high, mixing, kz, light, loss_rate, source):
    project, rebuild, turn = wave_tables()
    levels, species = tracers.shape[2:]
    hbm = pl.BlockSpec(memory_space=pltpu.HBM)
    f32 = jnp.float32
    dma = pltpu.SemaphoreType.DMA
    operands = (
        offsets,
        fraction,
        cutoffs,
        keep_high,
        mixing,
        light,
        tracers.reshape(CELLS, levels, species),
        kz.reshape(CELLS, levels).T,
        jnp.asarray(turn),
        jnp.asarray(project),
        jnp.asarray(rebuild),
        loss_rate,
        source,
    )
    out = pl.pallas_call(
        kernel,
        out_shape=pltpu.VMEM((CELLS, levels, species), f32),
        in_specs=[hbm] * 13,
        out_specs=pl.BlockSpec(memory_space=pltpu.VMEM),
        scratch_shapes=[
            pltpu.SMEM((1,), jnp.int32),
            pltpu.SMEM((1,), f32),
            pltpu.SMEM((1,), jnp.int32),
            pltpu.SMEM((1,), f32),
            pltpu.SMEM((1,), f32),
            pltpu.SMEM((1, CELLS), f32),
            pltpu.VMEM((levels, CELLS), f32),
            pltpu.VMEM(turn.shape, f32),
            pltpu.VMEM(project.shape, jnp.bfloat16),
            pltpu.VMEM(rebuild.shape, jnp.bfloat16),
            pltpu.VMEM((levels, species), f32),
            pltpu.VMEM((levels, species), f32),
            pltpu.VMEM((TILES, CELLS, 8, 128), f32),
            pltpu.VMEM((CELLS, 128), f32),
            pltpu.VMEM((CELLS, 128), f32),
            pltpu.VMEM((128, 128), f32),
            pltpu.VMEM((TILES, PEERS, CELLS, 128), f32),
            pltpu.VMEM((TILES, PEERS, CELLS, 128), f32),
            pltpu.VMEM((TILES, PEERS, CELLS, 128), f32),
            pltpu.VMEM((TILES, HALF + 2 * EDGE, 128), f32),
            pltpu.VMEM((TILES, EDGE + 2 * KPAD, 128), f32),
            pltpu.VMEM((TILES, EDGE + 2 * KPAD, 128), f32),
            pltpu.VMEM((3, TILES, HALF, 128), f32),
            pltpu.VMEM((TILES, DIRECT, 128), f32),
            pltpu.VMEM((TILES, PEERS, CELLS, 128), f32),
            dma((TILES,)),
            dma,
            dma((TILES,)),
            dma,
            dma,
            dma((TILES,)),
            dma((2,)),
            dma((2, 2, TILES)),
            dma,
            dma((TILES,)),
            dma,
            dma,
            dma((TILES,)),
            dma((12,)),
        ],
        compiler_params=pltpu.CompilerParams(
            collective_id=0, has_side_effects=True, vmem_limit_bytes=46 << 20
        ),
        name="transport",
    )(*[pltpu.with_memory_space_constraint(x, pltpu.HBM) if x.size > 1 else x for x in operands])
    return out.reshape(tracers.shape)


def solution(mesh):
    return jax.shard_map(
        body,
        mesh=mesh,
        in_specs=(
            P("lat", "lon", None, None),
            P("lat"),
            P("lat"),
            P("lat"),
            P("lat"),
            P("lat"),
            P("lat", "lon", None),
            P("lat", "lon"),
            P(),
            P(),
        ),
        out_specs=P("lat", "lon", None, None),
        check_vma=False,
    )
```

```python
import functools
import math

import jax
import jax.numpy as jnp
import numpy as np
from jax import lax
from jax.experimental import pallas as pl
from jax.experimental.pallas import tpu as pltpu
from jax.sharding import PartitionSpec as P

NLON = 1440
KMAX = 48
MESH = pl.DeviceIdType.MESH
CELLS = 90
PEERS = 8
HALF = CELLS * PEERS
LEVELS = 72
TILES = 9
EDGE = 184
KPAD = 56
DIRECT = HALF // 2
GROUP = PEERS // 2
RELAYED = ((3, 7), (7, 3), (7, 4), (4, 7), (4, 0), (0, 4), (0, 3), (3, 0))
LOW = 8
FULL = ((0, 2 * KPAD),)
CLASSES = (
    (0, 0, 48, FULL),
    (1, 2, 96, FULL),
    (3, 4, 136, FULL),
    (5, 6, EDGE, FULL),
    (7, 7, EDGE, ((0, LOW), (KPAD, LOW))),
)
LEFT = EDGE
RIGHT = EDGE + HALF


def split_bf16(table):
    import ml_dtypes

    high = table.astype(ml_dtypes.bfloat16)
    low = (table - high.astype(np.float64)).astype(ml_dtypes.bfloat16)
    return high, low


def wave_tables():
    places = np.arange(HALF)
    waves = np.arange(KMAX + 1)
    phase = (places[:, None] * waves[None, :] % NLON) * (2.0 * math.pi / NLON)
    table = np.zeros((HALF, 2 * KPAD))
    table[:, : KMAX + 1] = np.cos(phase)
    table[:, KPAD : KPAD + KMAX + 1] = np.sin(phase)
    high, low = split_bf16(table)
    rebuild = np.concatenate([high, low], axis=1)
    project = np.ascontiguousarray(rebuild.T)
    shifts = np.arange(-EDGE, EDGE)
    phase = (shifts[:, None] * waves[None, :] % NLON) * (2.0 * math.pi / NLON)
    turn = np.zeros((2 * EDGE, 128), np.float32)
    turn[:, : KMAX + 1] = np.cos(phase)
    turn[:, KPAD : KPAD + KMAX + 1] = np.sin(phase)
    return project, rebuild, turn


def kernel(
    off_hbm,
    frac_hbm,
    cut_hbm,
    keep_hbm,
    mix_hbm,
    light_hbm,
    tracers_ref,
    kz_hbm,
    turn_hbm,
    project_hbm,
    rebuild_hbm,
    loss_hbm,
    source_hbm,
    out_ref,
    off_ref,
    frac_ref,
    cut_ref,
    keep_ref,
    mix_ref,
    light_ref,
    kz_ref,
    turn_ref,
    project_ref,
    rebuild_ref,
    loss_ref,
    source_ref,
    inp,
    kbuf,
    glow,
    rot,
    dp,
    cp,
    got,
    circ,
    given,
    taken,
    rows,
    relay,
    back,
    in_sem,
    fs,
    fr,
    es,
    ss,
    er,
    ls,
    lr,
    rs,
    rr,
    os,
    bs,
    br,
    arg_sem,
):
    lon = lax.axis_index("lon")
    lat = lax.axis_index("lat")
    me = lon % PEERS
    base = lon - me
    other = {"lon": (lon + PEERS) % (2 * PEERS), "lat": lat}
    has_south = lat > 0
    has_north = lat < 7
    plain_south = has_south & (lat != 4)
    plain_north = has_north & (lat != 3)

    def peer(p):
        return {"lon": base + p, "lat": lat}

    def tile_in(j):
        return pltpu.make_async_copy(
            tracers_ref.at[:, pl.ds(pl.multiple_of(j * 8, 8), 8), :], inp.at[j], in_sem.at[j]
        )

    def forth(j, src, dst, to):
        return pltpu.make_async_remote_copy(
            dp.at[j, src], got.at[j, dst], fs, fr.at[j], device_id=peer(to), device_id_type=MESH
        )

    def home(j, src, dst, to):
        return pltpu.make_async_remote_copy(
            got.at[j, src], back.at[j, dst], bs, br.at[j], device_id=peer(to), device_id_type=MESH
        )

    def edge_copy(j, n):
        return pltpu.make_async_remote_copy(
            given.at[j, pl.ds(EDGE - n, n)], taken.at[j, pl.ds(EDGE - n, n)], es, er.at[j],
            device_id=other, device_id_type=MESH,
        )

    def spec_copy(j, first, count):
        part = pl.ds(EDGE + first, count)
        return pltpu.make_async_remote_copy(
            given.at[j, part], taken.at[j, part], ss, er.at[j],
            device_id=other, device_id_type=MESH,
        )

    def in_class(lo, hi):
        return (lat >= lo) & (lat <= hi)

    def half(h):
        return pl.ds(h * DIRECT, DIRECT)

    def row_copy(j, h, slot, to):
        return pltpu.make_async_remote_copy(
            rows.at[2, j, half(h)], rows.at[slot, j, half(h)], ls.at[slot], lr.at[slot, h, j],
            device_id={"lon": lon, "lat": to}, device_id_type=MESH,
        )

    def relay_copy(j, to):
        return pltpu.make_async_remote_copy(
            rows.at[2, j, half(1)], relay.at[j], rs, rr.at[j],
            device_id={"lon": lon, "lat": to}, device_id_type=MESH,
        )

    def onward_copy(j, slot, to):
        return pltpu.make_async_remote_copy(
            relay.at[j], rows.at[slot, j, half(1)], os, lr.at[slot, 1, j],
            device_id={"lon": lon, "lat": to}, device_id_type=MESH,
        )

    def start_in(j, carry):
        tile_in(j).start()
        return carry

    pairs = (
        (kz_hbm, kz_ref),
        (off_hbm, off_ref),
        (frac_hbm, frac_ref),
        (cut_hbm, cut_ref),
        (keep_hbm, keep_ref),
        (mix_hbm, mix_ref),
        (light_hbm, light_ref),
        (turn_hbm, turn_ref),
        (project_hbm, project_ref),
        (rebuild_hbm, rebuild_ref),
        (loss_hbm, loss_ref),
        (source_hbm, source_ref),
    )
    arrivals = [
        pltpu.make_async_copy(src, dst, arg_sem.at[n]) for n, (src, dst) in enumerate(pairs)
    ]
    arrivals[0].start()
    lax.fori_loop(0, TILES, start_in, 0)
    for copy in arrivals[1:]:
        copy.start()

    @pl.when(lat == 7)
    def _():
        for first, last in ((LOW, KPAD), (KPAD + LOW, 2 * KPAD)):
            taken[:, EDGE + first : EDGE + last, :] = jnp.zeros((TILES, last - first, 128), jnp.float32)

    barrier = pltpu.get_barrier_semaphore()
    for d in range(1, PEERS):
        pl.semaphore_signal(barrier, inc=1, device_id=peer((me + d) % PEERS), device_id_type=MESH)
    pl.semaphore_signal(barrier, inc=1, device_id=other, device_id_type=MESH)

    @pl.when(has_south)
    def _():
        pl.semaphore_signal(
            barrier, inc=1, device_id={"lon": lon, "lat": lat - 1}, device_id_type=MESH
        )

    @pl.when(has_north)
    def _():
        pl.semaphore_signal(
            barrier, inc=1, device_id={"lon": lon, "lat": lat + 1}, device_id_type=MESH
        )

    for here, there in RELAYED:

        @pl.when(lat == here)
        def _():
            pl.semaphore_signal(
                barrier, inc=1, device_id={"lon": lon, "lat": there}, device_id_type=MESH
            )

    arrivals[0].wait()
    rot[...] = jnp.zeros_like(rot)
    rot[0:72, 0:CELLS] = kz_ref[...]
    kbuf[...] = rot[...].T[0:CELLS, :]

    def down(j, carry):
        last, e, kc = carry
        tile_in(j).wait()
        flat = inp.at[j].reshape(CELLS * 8, 128)
        kr = pltpu.roll(kbuf[...], lax.rem(128 - 8 * j, 128), 1)
        for p in range(8):
            kn = jnp.broadcast_to(kr[:, p + 1 : p + 2], (CELLS, 128))
            g = 1.0 + kc * e
            inv = 1.0 / (g + kn)
            last = (flat[pl.ds(p, CELLS, stride=8), :] + kc * last) * inv
            e = g * inv
            dp[j, p] = last
            cp[j, p] = kn * inv
            kc = kn
        return last, e, kc

    zero = jnp.zeros((CELLS, 128), jnp.float32)
    lax.fori_loop(
        0, TILES, down, (zero, zero + 1.0, jnp.broadcast_to(kbuf[:, 0:1], (CELLS, 128)))
    )

    edge_row = (lat == 0) | (lat == 7)
    cross_row = (lat == 3) | (lat == 4)

    @pl.when(edge_row)
    def _():
        pl.semaphore_wait(barrier, PEERS + 3)

    @pl.when(cross_row)
    def _():
        pl.semaphore_wait(barrier, PEERS + 4)

    @pl.when(jnp.logical_not(edge_row | cross_row))
    def _():
        pl.semaphore_wait(barrier, PEERS + 2)

    def up(c, x):
        j = TILES - 1 - c
        for p in reversed(range(8)):
            x = dp[j, p] + cp[j, p] * x
            dp[j, p] = x

        @pl.when(c == 0)
        def _():
            send(j, 0)

        return x

    def send(j, core):
        for d in range(1, GROUP):
            to = (me // 2 + d) % GROUP * 2 + core
            forth(j, to, me, to).start()
        near = me // 2 * 2 + core

        @pl.when(near == me)
        def _():
            pltpu.make_async_copy(dp.at[j, me], got.at[j, me], fr.at[j]).start()

        @pl.when(near != me)
        def _():
            forth(j, near, me, near).start()

    lax.fori_loop(0, TILES, up, zero)

    for copy in arrivals[1:]:
        copy.wait()
    off = off_ref[0]
    frac = frac_ref[0]
    keep = keep_ref[0]
    mix = mix_ref[0]

    def light_row(c, carry):
        glow[pl.ds(c, 1), :] = jnp.full((1, 128), light_ref[0, c], jnp.float32)
        return carry

    lax.fori_loop(0, CELLS, light_row, 0)

    lane = lax.broadcasted_iota(jnp.int32, (1, 128), 1)
    wave = lane % KPAD
    share = jnp.where(wave <= cut_ref[0], jnp.where(wave == 0, 1.0, 2.0) / NLON, 0.0) * (1.0 - keep)
    turn = (1.0 - frac) * turn_ref[pl.ds(EDGE + off, 1), :] + frac * turn_ref[pl.ds(EDGE + 1 + off, 1), :]
    rot[...] = jnp.broadcast_to(turn * share, (128, 128)).T

    send(TILES - 1, 1)

    def gather(j):
        pltpu.make_async_copy(dp.at[j], got.at[j], fr.at[j]).wait()

        @pl.when(j == TILES - 1)
        def _():
            send(j - 1, 0)
            send(j - 1, 1)

        @pl.when(j >= 2)
        def _():
            send(j - 2, 0)
            send(j - 2, 1)

        for s in range(PEERS):
            circ[j, LEFT + CELLS * s : LEFT + CELLS * (s + 1), :] = got[j, s]
        for lo, hi, n, parts in CLASSES:

            @pl.when(in_class(lo, hi))
            def _():
                begin = jnp.clip(LEFT + (off + 1) * HALF, LEFT, RIGHT - n)
                given[j, EDGE - n : EDGE, :] = circ[j, pl.ds(begin, n), :]
                edge_copy(j, n).start()

        field = circ[j, LEFT:RIGHT, :]
        high = field.astype(jnp.bfloat16)
        low = (field - high.astype(jnp.float32)).astype(jnp.bfloat16)
        part = jnp.dot(
            project_ref[...], jnp.concatenate([high, low], axis=1), preferred_element_type=jnp.float32
        )
        n = 2 * KPAD
        given[j, EDGE : EDGE + n, :] = part[:n, :128] + part[n:, :128] + part[:n, 128:]
        for lo, hi, n, parts in CLASSES:

            @pl.when(in_class(lo, hi))
            def _():
                for first, count in parts:
                    spec_copy(j, first, count).start()

    def filt(j):
        for lo, hi, n, parts in CLASSES:

            @pl.when(in_class(lo, hi))
            def _():
                come = pl.ds(0, n + sum(count for _, count in parts))
                pltpu.make_async_copy(given.at[j, come], taken.at[j, come], er.at[j]).wait()
                fresh = taken[j, EDGE - n : EDGE, :]
                circ[j, LEFT - n : LEFT, :] = fresh
                circ[j, RIGHT : RIGHT + n, :] = fresh

        level = lax.broadcasted_iota(jnp.int32, (KPAD, 128), 0)
        sign = jnp.where(level % 2 == 0, 1.0, -1.0)
        cosine, sine = slice(EDGE, EDGE + KPAD), slice(EDGE + KPAD, EDGE + 2 * KPAD)
        a = given[j, cosine, :] + sign * taken[j, cosine, :]
        b = given[j, sine, :] + sign * taken[j, sine, :]
        c = rot[0:KPAD, :]
        d = rot[KPAD : 2 * KPAD, :]
        turned = jnp.concatenate([c * a - d * b, d * a + c * b], axis=0)
        high = turned.astype(jnp.bfloat16)
        low = (turned - high.astype(jnp.float32)).astype(jnp.bfloat16)
        weight = jnp.concatenate(
            [
                jnp.concatenate([high, low], axis=1),
                jnp.concatenate([high, jnp.zeros_like(low)], axis=1),
            ],
            axis=0,
        )
        for h in range(2):
            first = h * DIRECT
            lowpass = jnp.dot(
                rebuild_ref[first : first + DIRECT, :], weight, preferred_element_type=jnp.float32
            )
            near = circ[j, pl.ds(LEFT + first - off, DIRECT), :]
            far = circ[j, pl.ds(LEFT + first - 1 - off, DIRECT), :]
            moved = (1.0 - frac) * near + frac * far
            rows[2, j, first : first + DIRECT, :] = keep * moved + lowpass[:, :128] + lowpass[:, 128:]

            @pl.when(plain_north)
            def _():
                row_copy(j, h, 0, lat + 1).start()

            @pl.when(plain_south)
            def _():
                row_copy(j, h, 1, lat - 1).start()

            @pl.when(lat == 3)
            def _():
                (relay_copy(j, 7) if h else row_copy(j, 0, 0, 4)).start()

            @pl.when(lat == 4)
            def _():
                (relay_copy(j, 0) if h else row_copy(j, 0, 1, 3)).start()

    def onward(j):
        @pl.when(lat == 7)
        def _():
            relay_copy(j, 7).wait_recv()
            onward_copy(j, 0, 4).start()

        @pl.when(lat == 0)
        def _():
            relay_copy(j, 0).wait_recv()
            onward_copy(j, 1, 3).start()

    south_slot = jnp.where(has_south, 0, 2)
    north_slot = jnp.where(has_north, 1, 2)

    def spread(j):
        for h in range(2):

            @pl.when(has_south)
            def _():
                row_copy(j, h, 0, lat - 1).wait_recv()

            @pl.when(has_north)
            def _():
                row_copy(j, h, 1, lat + 1).wait_recv()

            for s in range(h * GROUP, (h + 1) * GROUP):
                part = pl.ds(CELLS * s, CELLS)
                got[j, s] = (1.0 - 2.0 * mix) * rows[2, j, part, :] + mix * (
                    rows[south_slot, j, part, :] + rows[north_slot, j, part, :]
                )
            for d in range(1, GROUP):
                to = h * GROUP + (me + d) % GROUP
                home(j, to, me, to).start()

            @pl.when(me // GROUP == h)
            def _():
                pltpu.make_async_copy(got.at[j, me], back.at[j, me], br.at[j]).start()

            @pl.when(me // GROUP != h)
            def _():
                to = h * GROUP + me % GROUP
                home(j, to, me, to).start()

    def finish(j):
        pltpu.make_async_copy(got.at[j], back.at[j], br.at[j]).wait()
        flat = out_ref.reshape(CELLS * LEVELS, 128)
        light = glow[...]
        for p in range(PEERS):
            level = j * 8 + p
            top = back[j, p] + source_ref[pl.ds(level, 1), :] * light
            flat[pl.ds(level, CELLS, stride=LEVELS), :] = top / (
                1.0 + loss_ref[pl.ds(level, 1), :] * light
            )

    stages = ((filt, 2), (gather, 0), (spread, 3), (onward, 2), (finish, 5))

    def step(t, carry):
        @pl.when(t == 1)
        def _():
            filt(TILES - 1)

        for stage, lag in stages:

            @pl.when((t >= lag + (stage is filt)) & (t < lag + TILES))
            def _():
                stage(TILES - 1 - (t - lag))

        return carry

    lax.fori_loop(0, TILES + 5, step, 0)

    sent = pl.ds(0, PEERS - 1)
    pltpu.make_async_copy(dp.at[:, sent], dp.at[:, sent], fs).wait()
    pltpu.make_async_copy(got.at[:, sent], got.at[:, sent], bs).wait()
    for lo, hi, n, parts in CLASSES:

        @pl.when(in_class(lo, hi))
        def _():
            edges = given.at[:, pl.ds(0, n)]
            spectra = given.at[:, pl.ds(0, sum(count for _, count in parts))]
            pltpu.make_async_copy(edges, edges, es).wait()
            pltpu.make_async_copy(spectra, spectra, ss).wait()

    whole, part = rows.at[2], rows.at[2, :, half(0)]

    @pl.when(plain_north)
    def _():
        pltpu.make_async_copy(whole, whole, ls.at[0]).wait()

    @pl.when(plain_south)
    def _():
        pltpu.make_async_copy(whole, whole, ls.at[1]).wait()

    @pl.when(lat == 3)
    def _():
        pltpu.make_async_copy(part, part, ls.at[0]).wait()

    @pl.when(lat == 4)
    def _():
        pltpu.make_async_copy(part, part, ls.at[1]).wait()

    @pl.when(cross_row)
    def _():
        pltpu.make_async_copy(relay, relay, rs).wait()

    @pl.when(edge_row)
    def _():
        pltpu.make_async_copy(relay, relay, os).wait()


def body(tracers, offsets, fraction, cutoffs, keep_high, mixing, kz, light, loss_rate, source):
    project, rebuild, turn = wave_tables()
    levels, species = tracers.shape[2:]
    hbm = pl.BlockSpec(memory_space=pltpu.HBM)
    f32 = jnp.float32
    dma = pltpu.SemaphoreType.DMA
    operands = (
        offsets,
        fraction,
        cutoffs,
        keep_high,
        mixing,
        light,
        tracers.reshape(CELLS, levels, species),
        kz.reshape(CELLS, levels).T,
        jnp.asarray(turn),
        jnp.asarray(project),
        jnp.asarray(rebuild),
        loss_rate,
        source,
    )
    out = pl.pallas_call(
        kernel,
        out_shape=pltpu.VMEM((CELLS, levels, species), f32),
        in_specs=[hbm] * 13,
        out_specs=pl.BlockSpec(memory_space=pltpu.VMEM),
        scratch_shapes=[
            pltpu.SMEM((1,), jnp.int32),
            pltpu.SMEM((1,), f32),
            pltpu.SMEM((1,), jnp.int32),
            pltpu.SMEM((1,), f32),
            pltpu.SMEM((1,), f32),
            pltpu.SMEM((1, CELLS), f32),
            pltpu.VMEM((levels, CELLS), f32),
            pltpu.VMEM(turn.shape, f32),
            pltpu.VMEM(project.shape, jnp.bfloat16),
            pltpu.VMEM(rebuild.shape, jnp.bfloat16),
            pltpu.VMEM((levels, species), f32),
            pltpu.VMEM((levels, species), f32),
            pltpu.VMEM((TILES, CELLS, 8, 128), f32),
            pltpu.VMEM((CELLS, 128), f32),
            pltpu.VMEM((CELLS, 128), f32),
            pltpu.VMEM((128, 128), f32),
            pltpu.VMEM((TILES, PEERS, CELLS, 128), f32),
            pltpu.VMEM((TILES, PEERS, CELLS, 128), f32),
            pltpu.VMEM((TILES, PEERS, CELLS, 128), f32),
            pltpu.VMEM((TILES, HALF + 2 * EDGE, 128), f32),
            pltpu.VMEM((TILES, EDGE + 2 * KPAD, 128), f32),
            pltpu.VMEM((TILES, EDGE + 2 * KPAD, 128), f32),
            pltpu.VMEM((3, TILES, HALF, 128), f32),
            pltpu.VMEM((TILES, DIRECT, 128), f32),
            pltpu.VMEM((TILES, PEERS, CELLS, 128), f32),
            dma((TILES,)),
            dma,
            dma((TILES,)),
            dma,
            dma,
            dma((TILES,)),
            dma((2,)),
            dma((2, 2, TILES)),
            dma,
            dma((TILES,)),
            dma,
            dma,
            dma((TILES,)),
            dma((12,)),
        ],
        compiler_params=pltpu.CompilerParams(
            collective_id=0, has_side_effects=True, vmem_limit_bytes=46 << 20
        ),
        name="transport",
    )(*[pltpu.with_memory_space_constraint(x, pltpu.HBM) if x.size > 1 else x for x in operands])
    return out.reshape(tracers.shape)


def solution(mesh):
    return jax.shard_map(
        body,
        mesh=mesh,
        in_specs=(
            P("lat", "lon", None, None),
            P("lat"),
            P("lat"),
            P("lat"),
            P("lat"),
            P("lat"),
            P("lat", "lon", None),
            P("lat", "lon"),
            P(),
            P(),
        ),
        out_specs=P("lat", "lon", None, None),
        check_vma=False,
    )
```

```python
import functools
import math

import jax
import jax.numpy as jnp
import numpy as np
from jax import lax
from jax.experimental import pallas as pl
from jax.experimental.pallas import tpu as pltpu
from jax.sharding import PartitionSpec as P

NLON = 1440
KMAX = 48
MESH = pl.DeviceIdType.MESH
CELLS = 90
PEERS = 8
HALF = CELLS * PEERS
LEVELS = 72
TILES = 9
EDGE = 184
KPAD = 56
DIRECT = HALF // 2
GROUP = PEERS // 2
RELAYED = ((3, 7), (7, 3), (7, 4), (4, 7), (4, 0), (0, 4), (0, 3), (3, 0))
LOW = 8
FULL = ((0, 2 * KPAD),)
CLASSES = (
    (0, 0, 48, FULL),
    (1, 2, 96, FULL),
    (3, 4, 136, FULL),
    (5, 6, EDGE, FULL),
    (7, 7, EDGE, ((0, LOW), (KPAD, LOW))),
)
LEFT = EDGE
RIGHT = EDGE + HALF


def split_bf16(table):
    import ml_dtypes

    high = table.astype(ml_dtypes.bfloat16)
    low = (table - high.astype(np.float64)).astype(ml_dtypes.bfloat16)
    return high, low


def wave_tables():
    places = np.arange(HALF)
    waves = np.arange(KMAX + 1)
    phase = (places[:, None] * waves[None, :] % NLON) * (2.0 * math.pi / NLON)
    table = np.zeros((HALF, 2 * KPAD))
    table[:, : KMAX + 1] = np.cos(phase)
    table[:, KPAD : KPAD + KMAX + 1] = np.sin(phase)
    high, low = split_bf16(table)
    rebuild = np.concatenate([high, low], axis=1)
    project = np.ascontiguousarray(rebuild.T)
    shifts = np.arange(-EDGE, EDGE)
    phase = (shifts[:, None] * waves[None, :] % NLON) * (2.0 * math.pi / NLON)
    turn = np.zeros((2 * EDGE, 128), np.float32)
    turn[:, : KMAX + 1] = np.cos(phase)
    turn[:, KPAD : KPAD + KMAX + 1] = np.sin(phase)
    return project, rebuild, turn


def kernel(
    off_hbm,
    frac_hbm,
    cut_hbm,
    keep_hbm,
    mix_hbm,
    light_hbm,
    tracers_ref,
    kz_hbm,
    turn_hbm,
    project_hbm,
    rebuild_hbm,
    loss_hbm,
    source_hbm,
    out_ref,
    off_ref,
    frac_ref,
    cut_ref,
    keep_ref,
    mix_ref,
    light_ref,
    kz_ref,
    turn_ref,
    project_ref,
    rebuild_ref,
    loss_ref,
    source_ref,
    inp,
    kbuf,
    glow,
    rot,
    dp,
    cp,
    got,
    circ,
    given,
    taken,
    rows,
    relay,
    back,
    in_sem,
    fs,
    fr,
    es,
    ss,
    er,
    ls,
    lr,
    rs,
    rr,
    os,
    bs,
    br,
    arg_sem,
):
    lon = lax.axis_index("lon")
    lat = lax.axis_index("lat")
    me = lon % PEERS
    base = lon - me
    other = {"lon": (lon + PEERS) % (2 * PEERS), "lat": lat}
    has_south = lat > 0
    has_north = lat < 7
    plain_south = has_south & (lat != 4)
    plain_north = has_north & (lat != 3)

    def peer(p):
        return {"lon": base + p, "lat": lat}

    def tile_in(j):
        return pltpu.make_async_copy(
            tracers_ref.at[:, pl.ds(pl.multiple_of(j * 8, 8), 8), :], inp.at[j], in_sem.at[j]
        )

    def forth(j, src, dst, to):
        return pltpu.make_async_remote_copy(
            dp.at[j, src], got.at[j, dst], fs, fr.at[j], device_id=peer(to), device_id_type=MESH
        )

    def home(j, src, dst, to):
        return pltpu.make_async_remote_copy(
            got.at[j, src], back.at[j, dst], bs, br.at[j], device_id=peer(to), device_id_type=MESH
        )

    def edge_copy(j, n):
        return pltpu.make_async_remote_copy(
            given.at[j, pl.ds(EDGE - n, n)], taken.at[j, pl.ds(EDGE - n, n)], es, er.at[j],
            device_id=other, device_id_type=MESH,
        )

    def spec_copy(j, first, count):
        part = pl.ds(EDGE + first, count)
        return pltpu.make_async_remote_copy(
            given.at[j, part], taken.at[j, part], ss, er.at[j],
            device_id=other, device_id_type=MESH,
        )

    def in_class(lo, hi):
        return (lat >= lo) & (lat <= hi)

    def half(h):
        return pl.ds(h * DIRECT, DIRECT)

    def row_copy(j, h, slot, to):
        return pltpu.make_async_remote_copy(
            rows.at[2, j, half(h)], rows.at[slot, j, half(h)], ls.at[slot], lr.at[slot, h, j],
            device_id={"lon": lon, "lat": to}, device_id_type=MESH,
        )

    def relay_copy(j, to):
        return pltpu.make_async_remote_copy(
            rows.at[2, j, half(1)], relay.at[j], rs, rr.at[j],
            device_id={"lon": lon, "lat": to}, device_id_type=MESH,
        )

    def onward_copy(j, slot, to):
        return pltpu.make_async_remote_copy(
            relay.at[j], rows.at[slot, j, half(1)], os, lr.at[slot, 1, j],
            device_id={"lon": lon, "lat": to}, device_id_type=MESH,
        )

    def start_in(j, carry):
        tile_in(j).start()
        return carry

    pairs = (
        (kz_hbm, kz_ref),
        (off_hbm, off_ref),
        (frac_hbm, frac_ref),
        (cut_hbm, cut_ref),
        (keep_hbm, keep_ref),
        (mix_hbm, mix_ref),
        (light_hbm, light_ref),
        (turn_hbm, turn_ref),
        (project_hbm, project_ref),
        (rebuild_hbm, rebuild_ref),
        (loss_hbm, loss_ref),
        (source_hbm, source_ref),
    )
    arrivals = [
        pltpu.make_async_copy(src, dst, arg_sem.at[n]) for n, (src, dst) in enumerate(pairs)
    ]
    arrivals[0].start()
    lax.fori_loop(0, TILES, start_in, 0)
    for copy in arrivals[1:]:
        copy.start()

    @pl.when(lat == 7)
    def _():
        for first, last in ((LOW, KPAD), (KPAD + LOW, 2 * KPAD)):
            taken[:, EDGE + first : EDGE + last, :] = jnp.zeros((TILES, last - first, 128), jnp.float32)

    barrier = pltpu.get_barrier_semaphore()
    for d in range(1, PEERS):
        pl.semaphore_signal(barrier, inc=1, device_id=peer((me + d) % PEERS), device_id_type=MESH)
    pl.semaphore_signal(barrier, inc=1, device_id=other, device_id_type=MESH)

    @pl.when(has_south)
    def _():
        pl.semaphore_signal(
            barrier, inc=1, device_id={"lon": lon, "lat": lat - 1}, device_id_type=MESH
        )

    @pl.when(has_north)
    def _():
        pl.semaphore_signal(
            barrier, inc=1, device_id={"lon": lon, "lat": lat + 1}, device_id_type=MESH
        )

    for here, there in RELAYED:

        @pl.when(lat == here)
        def _():
            pl.semaphore_signal(
                barrier, inc=1, device_id={"lon": lon, "lat": there}, device_id_type=MESH
            )

    arrivals[0].wait()
    rot[...] = jnp.zeros_like(rot)
    rot[0:72, 0:CELLS] = kz_ref[...]
    kbuf[...] = rot[...].T[0:CELLS, :]

    def down(j, carry):
        last, e, kc = carry
        tile_in(j).wait()
        flat = inp.at[j].reshape(CELLS * 8, 128)
        kr = pltpu.roll(kbuf[...], lax.rem(128 - 8 * j, 128), 1)
        for p in range(8):
            kn = jnp.broadcast_to(kr[:, p + 1 : p + 2], (CELLS, 128))
            g = 1.0 + kc * e
            inv = 1.0 / (g + kn)
            last = (flat[pl.ds(p, CELLS, stride=8), :] + kc * last) * inv
            e = g * inv
            dp[j, p] = last
            cp[j, p] = kn * inv
            kc = kn
        return last, e, kc

    zero = jnp.zeros((CELLS, 128), jnp.float32)
    lax.fori_loop(
        0, TILES, down, (zero, zero + 1.0, jnp.broadcast_to(kbuf[:, 0:1], (CELLS, 128)))
    )

    edge_row = (lat == 0) | (lat == 7)
    cross_row = (lat == 3) | (lat == 4)

    @pl.when(edge_row)
    def _():
        pl.semaphore_wait(barrier, PEERS + 3)

    @pl.when(cross_row)
    def _():
        pl.semaphore_wait(barrier, PEERS + 4)

    @pl.when(jnp.logical_not(edge_row | cross_row))
    def _():
        pl.semaphore_wait(barrier, PEERS + 2)

    def up(c, x):
        j = TILES - 1 - c
        for p in reversed(range(8)):
            x = dp[j, p] + cp[j, p] * x
            dp[j, p] = x

        @pl.when(c == 0)
        def _():
            send(j, 0)

        return x

    def send(j, core):
        for d in range(1, GROUP):
            to = (me // 2 + d) % GROUP * 2 + core
            forth(j, to, me, to).start()
        near = me // 2 * 2 + core

        @pl.when(near == me)
        def _():
            pltpu.make_async_copy(dp.at[j, me], got.at[j, me], fr.at[j]).start()

        @pl.when(near != me)
        def _():
            forth(j, near, me, near).start()

    lax.fori_loop(0, TILES, up, zero)
    send(TILES - 1, 1)

    for copy in arrivals[1:]:
        copy.wait()
    off = off_ref[0]
    frac = frac_ref[0]
    keep = keep_ref[0]
    mix = mix_ref[0]

    def light_row(c, carry):
        glow[pl.ds(c, 1), :] = jnp.full((1, 128), light_ref[0, c], jnp.float32)
        return carry

    lax.fori_loop(0, CELLS, light_row, 0)

    lane = lax.broadcasted_iota(jnp.int32, (1, 128), 1)
    wave = lane % KPAD
    share = jnp.where(wave <= cut_ref[0], jnp.where(wave == 0, 1.0, 2.0) / NLON, 0.0) * (1.0 - keep)
    turn = (1.0 - frac) * turn_ref[pl.ds(EDGE + off, 1), :] + frac * turn_ref[pl.ds(EDGE + 1 + off, 1), :]
    rot[...] = jnp.broadcast_to(turn * share, (128, 128)).T

    def gather(j):
        pltpu.make_async_copy(dp.at[j], got.at[j], fr.at[j]).wait()

        @pl.when(j == TILES - 1)
        def _():
            send(j - 1, 0)
            send(j - 1, 1)

        @pl.when(j >= 2)
        def _():
            send(j - 2, 0)
            send(j - 2, 1)

        for s in range(PEERS):
            circ[j, LEFT + CELLS * s : LEFT + CELLS * (s + 1), :] = got[j, s]
        for lo, hi, n, parts in CLASSES:

            @pl.when(in_class(lo, hi))
            def _():
                begin = jnp.clip(LEFT + (off + 1) * HALF, LEFT, RIGHT - n)
                given[j, EDGE - n : EDGE, :] = circ[j, pl.ds(begin, n), :]
                edge_copy(j, n).start()

        field = circ[j, LEFT:RIGHT, :]
        high = field.astype(jnp.bfloat16)
        low = (field - high.astype(jnp.float32)).astype(jnp.bfloat16)
        part = jnp.dot(
            project_ref[...], jnp.concatenate([high, low], axis=1), preferred_element_type=jnp.float32
        )
        n = 2 * KPAD
        given[j, EDGE : EDGE + n, :] = part[:n, :128] + part[n:, :128] + part[:n, 128:]
        for lo, hi, n, parts in CLASSES:

            @pl.when(in_class(lo, hi))
            def _():
                for first, count in parts:
                    spec_copy(j, first, count).start()

    def filt(j):
        for lo, hi, n, parts in CLASSES:

            @pl.when(in_class(lo, hi))
            def _():
                come = pl.ds(0, n + sum(count for _, count in parts))
                pltpu.make_async_copy(given.at[j, come], taken.at[j, come], er.at[j]).wait()
                fresh = taken[j, EDGE - n : EDGE, :]
                circ[j, LEFT - n : LEFT, :] = fresh
                circ[j, RIGHT : RIGHT + n, :] = fresh

        level = lax.broadcasted_iota(jnp.int32, (KPAD, 128), 0)
        sign = jnp.where(level % 2 == 0, 1.0, -1.0)
        cosine, sine = slice(EDGE, EDGE + KPAD), slice(EDGE + KPAD, EDGE + 2 * KPAD)
        a = given[j, cosine, :] + sign * taken[j, cosine, :]
        b = given[j, sine, :] + sign * taken[j, sine, :]
        c = rot[0:KPAD, :]
        d = rot[KPAD : 2 * KPAD, :]
        turned = jnp.concatenate([c * a - d * b, d * a + c * b], axis=0)
        high = turned.astype(jnp.bfloat16)
        low = (turned - high.astype(jnp.float32)).astype(jnp.bfloat16)
        weight = jnp.concatenate(
            [
                jnp.concatenate([high, low], axis=1),
                jnp.concatenate([high, jnp.zeros_like(low)], axis=1),
            ],
            axis=0,
        )
        for h in range(2):
            first = h * DIRECT
            lowpass = jnp.dot(
                rebuild_ref[first : first + DIRECT, :], weight, preferred_element_type=jnp.float32
            )
            near = circ[j, pl.ds(LEFT + first - off, DIRECT), :]
            far = circ[j, pl.ds(LEFT + first - 1 - off, DIRECT), :]
            moved = (1.0 - frac) * near + frac * far
            rows[2, j, first : first + DIRECT, :] = keep * moved + lowpass[:, :128] + lowpass[:, 128:]

            @pl.when(plain_north)
            def _():
                row_copy(j, h, 0, lat + 1).start()

            @pl.when(plain_south)
            def _():
                row_copy(j, h, 1, lat - 1).start()

            @pl.when(lat == 3)
            def _():
                (relay_copy(j, 7) if h else row_copy(j, 0, 0, 4)).start()

            @pl.when(lat == 4)
            def _():
                (relay_copy(j, 0) if h else row_copy(j, 0, 1, 3)).start()

    def onward(j):
        @pl.when(lat == 7)
        def _():
            relay_copy(j, 7).wait_recv()
            onward_copy(j, 0, 4).start()

        @pl.when(lat == 0)
        def _():
            relay_copy(j, 0).wait_recv()
            onward_copy(j, 1, 3).start()

    south_slot = jnp.where(has_south, 0, 2)
    north_slot = jnp.where(has_north, 1, 2)

    def spread(j):
        for h in range(2):

            @pl.when(has_south)
            def _():
                row_copy(j, h, 0, lat - 1).wait_recv()

            @pl.when(has_north)
            def _():
                row_copy(j, h, 1, lat + 1).wait_recv()

            for s in range(h * GROUP, (h + 1) * GROUP):
                part = pl.ds(CELLS * s, CELLS)
                got[j, s] = (1.0 - 2.0 * mix) * rows[2, j, part, :] + mix * (
                    rows[south_slot, j, part, :] + rows[north_slot, j, part, :]
                )
            for d in range(1, GROUP):
                to = h * GROUP + (me + d) % GROUP
                home(j, to, me, to).start()

            @pl.when(me // GROUP == h)
            def _():
                pltpu.make_async_copy(got.at[j, me], back.at[j, me], br.at[j]).start()

            @pl.when(me // GROUP != h)
            def _():
                to = h * GROUP + me % GROUP
                home(j, to, me, to).start()

    def finish(j):
        pltpu.make_async_copy(got.at[j], back.at[j], br.at[j]).wait()
        flat = out_ref.reshape(CELLS * LEVELS, 128)
        light = glow[...]
        for p in range(PEERS):
            level = j * 8 + p
            top = back[j, p] + source_ref[pl.ds(level, 1), :] * light
            flat[pl.ds(level, CELLS, stride=LEVELS), :] = top / (
                1.0 + loss_ref[pl.ds(level, 1), :] * light
            )

    stages = ((filt, 2), (gather, 0), (spread, 3), (onward, 2), (finish, 5))

    def step(t, carry):
        @pl.when(t == 1)
        def _():
            filt(TILES - 1)

        for stage, lag in stages:

            @pl.when((t >= lag + (stage is filt)) & (t < lag + TILES))
            def _():
                stage(TILES - 1 - (t - lag))

        return carry

    lax.fori_loop(0, TILES + 5, step, 0)

    sent = pl.ds(0, PEERS - 1)
    pltpu.make_async_copy(dp.at[:, sent], dp.at[:, sent], fs).wait()
    pltpu.make_async_copy(got.at[:, sent], got.at[:, sent], bs).wait()
    for lo, hi, n, parts in CLASSES:

        @pl.when(in_class(lo, hi))
        def _():
            edges = given.at[:, pl.ds(0, n)]
            spectra = given.at[:, pl.ds(0, sum(count for _, count in parts))]
            pltpu.make_async_copy(edges, edges, es).wait()
            pltpu.make_async_copy(spectra, spectra, ss).wait()

    whole, part = rows.at[2], rows.at[2, :, half(0)]

    @pl.when(plain_north)
    def _():
        pltpu.make_async_copy(whole, whole, ls.at[0]).wait()

    @pl.when(plain_south)
    def _():
        pltpu.make_async_copy(whole, whole, ls.at[1]).wait()

    @pl.when(lat == 3)
    def _():
        pltpu.make_async_copy(part, part, ls.at[0]).wait()

    @pl.when(lat == 4)
    def _():
        pltpu.make_async_copy(part, part, ls.at[1]).wait()

    @pl.when(cross_row)
    def _():
        pltpu.make_async_copy(relay, relay, rs).wait()

    @pl.when(edge_row)
    def _():
        pltpu.make_async_copy(relay, relay, os).wait()


def body(tracers, offsets, fraction, cutoffs, keep_high, mixing, kz, light, loss_rate, source):
    project, rebuild, turn = wave_tables()
    levels, species = tracers.shape[2:]
    hbm = pl.BlockSpec(memory_space=pltpu.HBM)
    f32 = jnp.float32
    dma = pltpu.SemaphoreType.DMA
    operands = (
        offsets,
        fraction,
        cutoffs,
        keep_high,
        mixing,
        light,
        tracers.reshape(CELLS, levels, species),
        kz.reshape(CELLS, levels).T,
        jnp.asarray(turn),
        jnp.asarray(project),
        jnp.asarray(rebuild),
        loss_rate,
        source,
    )
    out = pl.pallas_call(
        kernel,
        out_shape=pltpu.VMEM((CELLS, levels, species), f32),
        in_specs=[hbm] * 13,
        out_specs=pl.BlockSpec(memory_space=pltpu.VMEM),
        scratch_shapes=[
            pltpu.SMEM((1,), jnp.int32),
            pltpu.SMEM((1,), f32),
            pltpu.SMEM((1,), jnp.int32),
            pltpu.SMEM((1,), f32),
            pltpu.SMEM((1,), f32),
            pltpu.SMEM((1, CELLS), f32),
            pltpu.VMEM((levels, CELLS), f32),
            pltpu.VMEM(turn.shape, f32),
            pltpu.VMEM(project.shape, jnp.bfloat16),
            pltpu.VMEM(rebuild.shape, jnp.bfloat16),
            pltpu.VMEM((levels, species), f32),
            pltpu.VMEM((levels, species), f32),
            pltpu.VMEM((TILES, CELLS, 8, 128), f32),
            pltpu.VMEM((CELLS, 128), f32),
            pltpu.VMEM((CELLS, 128), f32),
            pltpu.VMEM((128, 128), f32),
            pltpu.VMEM((TILES, PEERS, CELLS, 128), f32),
            pltpu.VMEM((TILES, PEERS, CELLS, 128), f32),
            pltpu.VMEM((TILES, PEERS, CELLS, 128), f32),
            pltpu.VMEM((TILES, HALF + 2 * EDGE, 128), f32),
            pltpu.VMEM((TILES, EDGE + 2 * KPAD, 128), f32),
            pltpu.VMEM((TILES, EDGE + 2 * KPAD, 128), f32),
            pltpu.VMEM((3, TILES, HALF, 128), f32),
            pltpu.VMEM((TILES, DIRECT, 128), f32),
            pltpu.VMEM((TILES, PEERS, CELLS, 128), f32),
            dma((TILES,)),
            dma,
            dma((TILES,)),
            dma,
            dma,
            dma((TILES,)),
            dma((2,)),
            dma((2, 2, TILES)),
            dma,
            dma((TILES,)),
            dma,
            dma,
            dma((TILES,)),
            dma((12,)),
        ],
        compiler_params=pltpu.CompilerParams(
            collective_id=0, has_side_effects=True, vmem_limit_bytes=46 << 20
        ),
        name="transport",
    )(*[pltpu.with_memory_space_constraint(x, pltpu.HBM) if x.size > 1 else x for x in operands])
    return out.reshape(tracers.shape)


def solution(mesh):
    return jax.shard_map(
        body,
        mesh=mesh,
        in_specs=(
            P("lat", "lon", None, None),
            P("lat"),
            P("lat"),
            P("lat"),
            P("lat"),
            P("lat"),
            P("lat", "lon", None),
            P("lat", "lon"),
            P(),
            P(),
        ),
        out_specs=P("lat", "lon", None, None),
        check_vma=False,
    )
```

```python
import functools
import math

import jax
import jax.numpy as jnp
import numpy as np
from jax import lax
from jax.experimental import pallas as pl
from jax.experimental.pallas import tpu as pltpu
from jax.sharding import PartitionSpec as P

NLON = 1440
KMAX = 48
MESH = pl.DeviceIdType.MESH
CELLS = 90
PEERS = 8
HALF = CELLS * PEERS
LEVELS = 72
TILES = 9
EDGE = 184
KPAD = 56
DIRECT = HALF // 2
GROUP = PEERS // 2
RELAYED = ((3, 7), (7, 3), (7, 4), (4, 7), (4, 0), (0, 4), (0, 3), (3, 0))
LOW = 8
FULL = ((0, 2 * KPAD),)
CLASSES = (
    (0, 0, 48, FULL),
    (1, 2, 96, FULL),
    (3, 4, 136, FULL),
    (5, 5, 160, FULL),
    (6, 6, EDGE, FULL),
    (7, 7, EDGE, ((0, LOW), (KPAD, LOW))),
)
LEFT = EDGE
RIGHT = EDGE + HALF


def split_bf16(table):
    import ml_dtypes

    high = table.astype(ml_dtypes.bfloat16)
    low = (table - high.astype(np.float64)).astype(ml_dtypes.bfloat16)
    return high, low


def wave_tables():
    places = np.arange(HALF)
    waves = np.arange(KMAX + 1)
    phase = (places[:, None] * waves[None, :] % NLON) * (2.0 * math.pi / NLON)
    table = np.zeros((HALF, 2 * KPAD))
    table[:, : KMAX + 1] = np.cos(phase)
    table[:, KPAD : KPAD + KMAX + 1] = np.sin(phase)
    high, low = split_bf16(table)
    rebuild = np.concatenate([high, low], axis=1)
    project = np.ascontiguousarray(rebuild.T)
    shifts = np.arange(-EDGE, EDGE)
    phase = (shifts[:, None] * waves[None, :] % NLON) * (2.0 * math.pi / NLON)
    turn = np.zeros((2 * EDGE, 128), np.float32)
    turn[:, : KMAX + 1] = np.cos(phase)
    turn[:, KPAD : KPAD + KMAX + 1] = np.sin(phase)
    return project, rebuild, turn


def kernel(
    off_hbm,
    frac_hbm,
    cut_hbm,
    keep_hbm,
    mix_hbm,
    light_hbm,
    tracers_ref,
    kz_hbm,
    turn_hbm,
    project_hbm,
    rebuild_hbm,
    loss_hbm,
    source_hbm,
    out_ref,
    off_ref,
    frac_ref,
    cut_ref,
    keep_ref,
    mix_ref,
    light_ref,
    kz_ref,
    turn_ref,
    project_ref,
    rebuild_ref,
    loss_ref,
    source_ref,
    inp,
    kbuf,
    glow,
    rot,
    dp,
    cp,
    got,
    circ,
    given,
    taken,
    rows,
    relay,
    back,
    in_sem,
    fs,
    fr,
    es,
    ss,
    er,
    ls,
    lr,
    rs,
    rr,
    os,
    bs,
    br,
    arg_sem,
):
    lon = lax.axis_index("lon")
    lat = lax.axis_index("lat")
    me = lon % PEERS
    base = lon - me
    other = {"lon": (lon + PEERS) % (2 * PEERS), "lat": lat}
    has_south = lat > 0
    has_north = lat < 7
    plain_south = has_south & (lat != 4)
    plain_north = has_north & (lat != 3)

    def peer(p):
        return {"lon": base + p, "lat": lat}

    def tile_in(j):
        return pltpu.make_async_copy(
            tracers_ref.at[:, pl.ds(pl.multiple_of(j * 8, 8), 8), :], inp.at[j], in_sem.at[j]
        )

    def forth(j, src, dst, to):
        return pltpu.make_async_remote_copy(
            dp.at[j, src], got.at[j, dst], fs, fr.at[j], device_id=peer(to), device_id_type=MESH
        )

    def home(j, src, dst, to):
        return pltpu.make_async_remote_copy(
            got.at[j, src], back.at[j, dst], bs, br.at[j], device_id=peer(to), device_id_type=MESH
        )

    def edge_copy(j, n):
        return pltpu.make_async_remote_copy(
            given.at[j, pl.ds(EDGE - n, n)], taken.at[j, pl.ds(EDGE - n, n)], es, er.at[j],
            device_id=other, device_id_type=MESH,
        )

    def spec_copy(j, first, count):
        part = pl.ds(EDGE + first, count)
        return pltpu.make_async_remote_copy(
            given.at[j, part], taken.at[j, part], ss, er.at[j],
            device_id=other, device_id_type=MESH,
        )

    def in_class(lo, hi):
        return (lat >= lo) & (lat <= hi)

    def half(h):
        return pl.ds(h * DIRECT, DIRECT)

    def row_copy(j, h, slot, to):
        return pltpu.make_async_remote_copy(
            rows.at[2, j, half(h)], rows.at[slot, j, half(h)], ls.at[slot], lr.at[slot, h, j],
            device_id={"lon": lon, "lat": to}, device_id_type=MESH,
        )

    def relay_copy(j, to):
        return pltpu.make_async_remote_copy(
            rows.at[2, j, half(1)], relay.at[j], rs, rr.at[j],
            device_id={"lon": lon, "lat": to}, device_id_type=MESH,
        )

    def onward_copy(j, slot, to):
        return pltpu.make_async_remote_copy(
            relay.at[j], rows.at[slot, j, half(1)], os, lr.at[slot, 1, j],
            device_id={"lon": lon, "lat": to}, device_id_type=MESH,
        )

    def start_in(j, carry):
        tile_in(j).start()
        return carry

    pairs = (
        (kz_hbm, kz_ref),
        (off_hbm, off_ref),
        (frac_hbm, frac_ref),
        (cut_hbm, cut_ref),
        (keep_hbm, keep_ref),
        (mix_hbm, mix_ref),
        (light_hbm, light_ref),
        (turn_hbm, turn_ref),
        (project_hbm, project_ref),
        (rebuild_hbm, rebuild_ref),
        (loss_hbm, loss_ref),
        (source_hbm, source_ref),
    )
    arrivals = [
        pltpu.make_async_copy(src, dst, arg_sem.at[n]) for n, (src, dst) in enumerate(pairs)
    ]
    arrivals[0].start()
    lax.fori_loop(0, TILES, start_in, 0)
    for copy in arrivals[1:]:
        copy.start()

    @pl.when(lat == 7)
    def _():
        for first, last in ((LOW, KPAD), (KPAD + LOW, 2 * KPAD)):
            taken[:, EDGE + first : EDGE + last, :] = jnp.zeros((TILES, last - first, 128), jnp.float32)

    barrier = pltpu.get_barrier_semaphore()
    for d in range(1, PEERS):
        pl.semaphore_signal(barrier, inc=1, device_id=peer((me + d) % PEERS), device_id_type=MESH)
    pl.semaphore_signal(barrier, inc=1, device_id=other, device_id_type=MESH)

    @pl.when(has_south)
    def _():
        pl.semaphore_signal(
            barrier, inc=1, device_id={"lon": lon, "lat": lat - 1}, device_id_type=MESH
        )

    @pl.when(has_north)
    def _():
        pl.semaphore_signal(
            barrier, inc=1, device_id={"lon": lon, "lat": lat + 1}, device_id_type=MESH
        )

    for here, there in RELAYED:

        @pl.when(lat == here)
        def _():
            pl.semaphore_signal(
                barrier, inc=1, device_id={"lon": lon, "lat": there}, device_id_type=MESH
            )

    arrivals[0].wait()
    rot[...] = jnp.zeros_like(rot)
    rot[0:72, 0:CELLS] = kz_ref[...]
    kbuf[...] = rot[...].T[0:CELLS, :]

    def down(j, carry):
        last, e, kc = carry
        tile_in(j).wait()
        flat = inp.at[j].reshape(CELLS * 8, 128)
        kr = pltpu.roll(kbuf[...], lax.rem(128 - 8 * j, 128), 1)
        for p in range(8):
            kn = jnp.broadcast_to(kr[:, p + 1 : p + 2], (CELLS, 128))
            g = 1.0 + kc * e
            inv = 1.0 / (g + kn)
            last = (flat[pl.ds(p, CELLS, stride=8), :] + kc * last) * inv
            e = g * inv
            dp[j, p] = last
            cp[j, p] = kn * inv
            kc = kn
        return last, e, kc

    zero = jnp.zeros((CELLS, 128), jnp.float32)
    lax.fori_loop(
        0, TILES, down, (zero, zero + 1.0, jnp.broadcast_to(kbuf[:, 0:1], (CELLS, 128)))
    )

    edge_row = (lat == 0) | (lat == 7)
    cross_row = (lat == 3) | (lat == 4)

    @pl.when(edge_row)
    def _():
        pl.semaphore_wait(barrier, PEERS + 3)

    @pl.when(cross_row)
    def _():
        pl.semaphore_wait(barrier, PEERS + 4)

    @pl.when(jnp.logical_not(edge_row | cross_row))
    def _():
        pl.semaphore_wait(barrier, PEERS + 2)

    def up(c, x):
        j = TILES - 1 - c
        for p in reversed(range(8)):
            x = dp[j, p] + cp[j, p] * x
            dp[j, p] = x

        @pl.when(c == 0)
        def _():
            send(j, 0)

        return x

    def send(j, core):
        for d in range(1, GROUP):
            to = (me // 2 + d) % GROUP * 2 + core
            forth(j, to, me, to).start()
        near = me // 2 * 2 + core

        @pl.when(near == me)
        def _():
            pltpu.make_async_copy(dp.at[j, me], got.at[j, me], fr.at[j]).start()

        @pl.when(near != me)
        def _():
            forth(j, near, me, near).start()

    lax.fori_loop(0, TILES, up, zero)

    for copy in arrivals[1:]:
        copy.wait()
    off = off_ref[0]
    frac = frac_ref[0]
    keep = keep_ref[0]
    mix = mix_ref[0]

    def light_row(c, carry):
        glow[pl.ds(c, 1), :] = jnp.full((1, 128), light_ref[0, c], jnp.float32)
        return carry

    lax.fori_loop(0, CELLS, light_row, 0)

    lane = lax.broadcasted_iota(jnp.int32, (1, 128), 1)
    wave = lane % KPAD
    share = jnp.where(wave <= cut_ref[0], jnp.where(wave == 0, 1.0, 2.0) / NLON, 0.0) * (1.0 - keep)
    turn = (1.0 - frac) * turn_ref[pl.ds(EDGE + off, 1), :] + frac * turn_ref[pl.ds(EDGE + 1 + off, 1), :]
    rot[...] = jnp.broadcast_to(turn * share, (128, 128)).T

    send(TILES - 1, 1)

    def gather(j):
        pltpu.make_async_copy(dp.at[j], got.at[j], fr.at[j]).wait()

        @pl.when(j == TILES - 1)
        def _():
            send(j - 1, 0)
            send(j - 1, 1)

        @pl.when(j >= 2)
        def _():
            send(j - 2, 0)
            send(j - 2, 1)

        for s in range(PEERS):
            circ[j, LEFT + CELLS * s : LEFT + CELLS * (s + 1), :] = got[j, s]
        for lo, hi, n, parts in CLASSES:

            @pl.when(in_class(lo, hi))
            def _():
                begin = jnp.clip(LEFT + (off + 1) * HALF, LEFT, RIGHT - n)
                given[j, EDGE - n : EDGE, :] = circ[j, pl.ds(begin, n), :]
                edge_copy(j, n).start()

        field = circ[j, LEFT:RIGHT, :]
        high = field.astype(jnp.bfloat16)
        low = (field - high.astype(jnp.float32)).astype(jnp.bfloat16)
        part = jnp.dot(
            project_ref[...], jnp.concatenate([high, low], axis=1), preferred_element_type=jnp.float32
        )
        n = 2 * KPAD
        given[j, EDGE : EDGE + n, :] = part[:n, :128] + part[n:, :128] + part[:n, 128:]
        for lo, hi, n, parts in CLASSES:

            @pl.when(in_class(lo, hi))
            def _():
                for first, count in parts:
                    spec_copy(j, first, count).start()

    def filt(j):
        for lo, hi, n, parts in CLASSES:

            @pl.when(in_class(lo, hi))
            def _():
                come = pl.ds(0, n + sum(count for _, count in parts))
                pltpu.make_async_copy(given.at[j, come], taken.at[j, come], er.at[j]).wait()
                fresh = taken[j, EDGE - n : EDGE, :]
                circ[j, LEFT - n : LEFT, :] = fresh
                circ[j, RIGHT : RIGHT + n, :] = fresh

        level = lax.broadcasted_iota(jnp.int32, (KPAD, 128), 0)
        sign = jnp.where(level % 2 == 0, 1.0, -1.0)
        cosine, sine = slice(EDGE, EDGE + KPAD), slice(EDGE + KPAD, EDGE + 2 * KPAD)
        a = given[j, cosine, :] + sign * taken[j, cosine, :]
        b = given[j, sine, :] + sign * taken[j, sine, :]
        c = rot[0:KPAD, :]
        d = rot[KPAD : 2 * KPAD, :]
        turned = jnp.concatenate([c * a - d * b, d * a + c * b], axis=0)
        high = turned.astype(jnp.bfloat16)
        low = (turned - high.astype(jnp.float32)).astype(jnp.bfloat16)
        weight = jnp.concatenate(
            [
                jnp.concatenate([high, low], axis=1),
                jnp.concatenate([high, jnp.zeros_like(low)], axis=1),
            ],
            axis=0,
        )
        for h in range(2):
            first = h * DIRECT
            lowpass = jnp.dot(
                rebuild_ref[first : first + DIRECT, :], weight, preferred_element_type=jnp.float32
            )
            near = circ[j, pl.ds(LEFT + first - off, DIRECT), :]
            far = circ[j, pl.ds(LEFT + first - 1 - off, DIRECT), :]
            moved = (1.0 - frac) * near + frac * far
            rows[2, j, first : first + DIRECT, :] = keep * moved + lowpass[:, :128] + lowpass[:, 128:]

            @pl.when(plain_north)
            def _():
                row_copy(j, h, 0, lat + 1).start()

            @pl.when(plain_south)
            def _():
                row_copy(j, h, 1, lat - 1).start()

            @pl.when(lat == 3)
            def _():
                (relay_copy(j, 7) if h else row_copy(j, 0, 0, 4)).start()

            @pl.when(lat == 4)
            def _():
                (relay_copy(j, 0) if h else row_copy(j, 0, 1, 3)).start()

    def onward(j):
        @pl.when(lat == 7)
        def _():
            relay_copy(j, 7).wait_recv()
            onward_copy(j, 0, 4).start()

        @pl.when(lat == 0)
        def _():
            relay_copy(j, 0).wait_recv()
            onward_copy(j, 1, 3).start()

    south_slot = jnp.where(has_south, 0, 2)
    north_slot = jnp.where(has_north, 1, 2)

    def spread(j):
        for h in range(2):

            @pl.when(has_south)
            def _():
                row_copy(j, h, 0, lat - 1).wait_recv()

            @pl.when(has_north)
            def _():
                row_copy(j, h, 1, lat + 1).wait_recv()

            for s in range(h * GROUP, (h + 1) * GROUP):
                part = pl.ds(CELLS * s, CELLS)
                got[j, s] = (1.0 - 2.0 * mix) * rows[2, j, part, :] + mix * (
                    rows[south_slot, j, part, :] + rows[north_slot, j, part, :]
                )
            for d in range(1, GROUP):
                to = h * GROUP + (me + d) % GROUP
                home(j, to, me, to).start()

            @pl.when(me // GROUP == h)
            def _():
                pltpu.make_async_copy(got.at[j, me], back.at[j, me], br.at[j]).start()

            @pl.when(me // GROUP != h)
            def _():
                to = h * GROUP + me % GROUP
                home(j, to, me, to).start()

    def finish(j):
        pltpu.make_async_copy(got.at[j], back.at[j], br.at[j]).wait()
        flat = out_ref.reshape(CELLS * LEVELS, 128)
        light = glow[...]
        for p in range(PEERS):
            level = j * 8 + p
            top = back[j, p] + source_ref[pl.ds(level, 1), :] * light
            flat[pl.ds(level, CELLS, stride=LEVELS), :] = top / (
                1.0 + loss_ref[pl.ds(level, 1), :] * light
            )

    stages = ((filt, 2), (gather, 0), (spread, 3), (onward, 2), (finish, 5))

    def step(t, carry):
        @pl.when(t == 1)
        def _():
            filt(TILES - 1)

        for stage, lag in stages:

            @pl.when((t >= lag + (stage is filt)) & (t < lag + TILES))
            def _():
                stage(TILES - 1 - (t - lag))

        return carry

    lax.fori_loop(0, TILES + 5, step, 0)

    sent = pl.ds(0, PEERS - 1)
    pltpu.make_async_copy(dp.at[:, sent], dp.at[:, sent], fs).wait()
    pltpu.make_async_copy(got.at[:, sent], got.at[:, sent], bs).wait()
    for lo, hi, n, parts in CLASSES:

        @pl.when(in_class(lo, hi))
        def _():
            edges = given.at[:, pl.ds(0, n)]
            spectra = given.at[:, pl.ds(0, sum(count for _, count in parts))]
            pltpu.make_async_copy(edges, edges, es).wait()
            pltpu.make_async_copy(spectra, spectra, ss).wait()

    whole, part = rows.at[2], rows.at[2, :, half(0)]

    @pl.when(plain_north)
    def _():
        pltpu.make_async_copy(whole, whole, ls.at[0]).wait()

    @pl.when(plain_south)
    def _():
        pltpu.make_async_copy(whole, whole, ls.at[1]).wait()

    @pl.when(lat == 3)
    def _():
        pltpu.make_async_copy(part, part, ls.at[0]).wait()

    @pl.when(lat == 4)
    def _():
        pltpu.make_async_copy(part, part, ls.at[1]).wait()

    @pl.when(cross_row)
    def _():
        pltpu.make_async_copy(relay, relay, rs).wait()

    @pl.when(edge_row)
    def _():
        pltpu.make_async_copy(relay, relay, os).wait()


def body(tracers, offsets, fraction, cutoffs, keep_high, mixing, kz, light, loss_rate, source):
    project, rebuild, turn = wave_tables()
    levels, species = tracers.shape[2:]
    hbm = pl.BlockSpec(memory_space=pltpu.HBM)
    f32 = jnp.float32
    dma = pltpu.SemaphoreType.DMA
    operands = (
        offsets,
        fraction,
        cutoffs,
        keep_high,
        mixing,
        light,
        tracers.reshape(CELLS, levels, species),
        kz.reshape(CELLS, levels).T,
        jnp.asarray(turn),
        jnp.asarray(project),
        jnp.asarray(rebuild),
        loss_rate,
        source,
    )
    out = pl.pallas_call(
        kernel,
        out_shape=pltpu.VMEM((CELLS, levels, species), f32),
        in_specs=[hbm] * 13,
        out_specs=pl.BlockSpec(memory_space=pltpu.VMEM),
        scratch_shapes=[
            pltpu.SMEM((1,), jnp.int32),
            pltpu.SMEM((1,), f32),
            pltpu.SMEM((1,), jnp.int32),
            pltpu.SMEM((1,), f32),
            pltpu.SMEM((1,), f32),
            pltpu.SMEM((1, CELLS), f32),
            pltpu.VMEM((levels, CELLS), f32),
            pltpu.VMEM(turn.shape, f32),
            pltpu.VMEM(project.shape, jnp.bfloat16),
            pltpu.VMEM(rebuild.shape, jnp.bfloat16),
            pltpu.VMEM((levels, species), f32),
            pltpu.VMEM((levels, species), f32),
            pltpu.VMEM((TILES, CELLS, 8, 128), f32),
            pltpu.VMEM((CELLS, 128), f32),
            pltpu.VMEM((CELLS, 128), f32),
            pltpu.VMEM((128, 128), f32),
            pltpu.VMEM((TILES, PEERS, CELLS, 128), f32),
            pltpu.VMEM((TILES, PEERS, CELLS, 128), f32),
            pltpu.VMEM((TILES, PEERS, CELLS, 128), f32),
            pltpu.VMEM((TILES, HALF + 2 * EDGE, 128), f32),
            pltpu.VMEM((TILES, EDGE + 2 * KPAD, 128), f32),
            pltpu.VMEM((TILES, EDGE + 2 * KPAD, 128), f32),
            pltpu.VMEM((3, TILES, HALF, 128), f32),
            pltpu.VMEM((TILES, DIRECT, 128), f32),
            pltpu.VMEM((TILES, PEERS, CELLS, 128), f32),
            dma((TILES,)),
            dma,
            dma((TILES,)),
            dma,
            dma,
            dma((TILES,)),
            dma((2,)),
            dma((2, 2, TILES)),
            dma,
            dma((TILES,)),
            dma,
            dma,
            dma((TILES,)),
            dma((12,)),
        ],
        compiler_params=pltpu.CompilerParams(
            collective_id=0, has_side_effects=True, vmem_limit_bytes=46 << 20
        ),
        name="transport",
    )(*[pltpu.with_memory_space_constraint(x, pltpu.HBM) if x.size > 1 else x for x in operands])
    return out.reshape(tracers.shape)


def solution(mesh):
    return jax.shard_map(
        body,
        mesh=mesh,
        in_specs=(
            P("lat", "lon", None, None),
            P("lat"),
            P("lat"),
            P("lat"),
            P("lat"),
            P("lat"),
            P("lat", "lon", None),
            P("lat", "lon"),
            P(),
            P(),
        ),
        out_specs=P("lat", "lon", None, None),
        check_vma=False,
    )
```
